32 devices in a mesh: task: 4 (over z), row: 2 (over x), col: 4 (over y, core).
Axes of the slice: x: 2, y: 2, z: 4, core: 2. Of those that a mesh axis runs over, the one named last changes fastest.
Arguments:
- activations: bfloat16 [4, 512, 13824], P('task', 'col', 'row'), may hold values from -6 to 6
- weights: bfloat16 [4, 13824, 5120], P('task', 'row', 'col'), may hold values from -0.0625 to 0.0625
- labels: int32 [4, 512], P('task'), may hold values from 0 to 127
- prototypes: bfloat16 [4, 128, 5120], P('task', None, 'col'), may hold values from -6 to 6
Outputs:
- merged: bfloat16 [13824, 5120], P('row', 'col')
- merged_out: bfloat16 [4, 512, 5120], P('task', 'row', 'col')
The draws below stay inside these ranges and needn't reach their ends.
All inputs are finite; a program needn't handle non-finite values.
Results may differ from the reference program's by a relative error of at most 0.02.
Values may be sent and summed in bfloat16 or wider, within the bound.
No kernel may reach another device: no remote copies, remote signals or barrier semaphores. Data moves between devices by JAX's collectives and lax.ppermute only.
A program may use at most 192 MiB of HBM per device.

```python
import jax
import jax.numpy as jnp
from jax import lax

D = 5120
FF = 13824
CLASSES = 128
TOK = 512
TASKS = 4


def plant(array, own_key, least, high):
    longest = array.shape.index(max(array.shape))
    spots = []
    for shift in (0, 1):
        where = [jax.random.randint(jax.random.fold_in(own_key, axis), (), 0, length) for axis, length in enumerate(array.shape)]
        where[longest] = (where[longest] + shift) % array.shape[longest]
        spots.append(tuple(where))
    return array.at[spots[0]].set(least).at[spots[1]].set(high)


def strengthened(values, own_key, source, target, blocks, factor):
    def block_of(position):
        return (jnp.arange(values.shape[position]) // (values.shape[position] // blocks)).reshape((-1,) + (1,) * (values.ndim - 1 - position))

    near = jax.random.permutation(own_key, blocks)[block_of(target)]
    second = (block_of(target) + blocks // 2) % blocks
    return jnp.where((block_of(source) == near) | (block_of(source) == second), factor * values, values)


def steps_of(stream_key, extent, shards, smallest, high):
    def one(position, parts):
        steps = jax.random.uniform(jax.random.fold_in(jax.random.fold_in(stream_key, 6), position), (parts,), jnp.float32, smallest / len(shards), high / len(shards))
        return jnp.repeat(jnp.exp(steps), extent[position] // parts).reshape((-1,) + (1,) * (len(extent) - position - 1))

    loudness = one(*shards[0])
    for cut in shards[1:]:
        loudness = loudness * one(*cut)
    return loudness


def noise(own_key, extent, deviation, reach, pieces=(), kind=jnp.bfloat16):
    gain = steps_of(own_key, extent, pieces, -0.22, 0.18) if pieces else 1.0
    drawn = jax.random.normal(own_key, extent, jnp.float32) * deviation * gain
    return jnp.minimum(jnp.maximum(drawn, -reach), reach).astype(kind)


def gaussian_with(key, extent, spread, reach, split, heavy, kind=jnp.bfloat16):
    values = spread * jax.random.normal(key, extent, jnp.float32)
    if split:
        values = values * steps_of(key, extent, split, -0.22, 0.18)
    return jnp.clip(strengthened(values, jax.random.fold_in(key, 3), *heavy), -reach, reach).astype(kind)


def setup_inputs(seed: int = 0) -> dict:
    arg_keys = jax.random.split(jax.random.key(seed), 5)
    return {
        "activations": noise(arg_keys[0], (TASKS, TOK, FF), 1.0, 6.0, ((0, 4), (1, 4), (2, 2))),
        "weights": gaussian_with(arg_keys[1], (TASKS, FF, D), FF ** -0.5, 0.0625, ((0, 4), (1, 2), (2, 4)), (0, 1, 4, 2.0)),
        "labels": plant(jax.random.randint(arg_keys[2], (TASKS, TOK), 0, CLASSES), jax.random.fold_in(arg_keys[2], 1), 0, CLASSES - 1).astype(jnp.int32),
        "prototypes": noise(arg_keys[3], (TASKS, CLASSES, D), 1.0, 6.0, ((0, 4), (2, 4))),
    }


def reference(activations, weights, labels, prototypes):
    def accumulate(carry, items):
        acts, weight, label_row, protos = items
        output = jnp.dot(acts, weight, preferred_element_type=jnp.float32)
        onehot = (label_row[:, None] == jnp.arange(CLASSES, dtype=jnp.int32)[None, :]).astype(jnp.bfloat16)
        target = jnp.dot(onehot, protos, preferred_element_type=jnp.float32)
        grad = output - target
        gsq = (grad * grad).astype(jnp.bfloat16)
        wide = acts.astype(jnp.float32)
        asq = (wide * wide).astype(jnp.bfloat16)
        fisher = jnp.dot(asq.T, gsq, preferred_element_type=jnp.float32)
        numer, denom = carry
        return (numer + fisher * weight.astype(jnp.float32), denom + fisher), None

    start = (jnp.zeros((FF, D), jnp.float32), jnp.zeros((FF, D), jnp.float32))
    (numer, denom), _ = lax.scan(accumulate, start, (activations, weights, labels, prototypes))
    merged = (numer / (denom + 1e-6)).astype(jnp.bfloat16)
    merged_out = lax.map(lambda acts: jnp.dot(acts, merged, preferred_element_type=jnp.float32).astype(jnp.bfloat16), activations)
    return merged, merged_out
```

```python
import functools

import jax
import jax.numpy as jnp
from jax import lax
from jax.experimental import pallas as pl
from jax.experimental.pallas import tpu as pltpu
from jax.sharding import PartitionSpec as P

BF16 = jnp.bfloat16
F32 = jnp.float32
ANY = pl.BlockSpec(memory_space=pl.ANY)
WIDTH = 256
UNIT_ROWS = 384
MOST = 3
LEAST = 1
LAG = 2
VMEM_LIMIT = 60 * 1024 * 1024
COST = pl.CostEstimate(flops=0, bytes_accessed=0, transcendentals=0)


def largest_divisor(total, limit, unit):
    best = total
    for size in range(unit, limit + 1, unit):
        if total % size == 0:
            best = size
    return best


def group_product(lhs, mat, group, groups, deps=()):
    tokens, rows = lhs.shape
    depth = largest_divisor(rows, 1152, 128)
    steps = rows // depth

    def body(lhs_ref, *rest):
        mats, (out_ref, acc_ref) = rest[:groups], rest[-2:]
        step = pl.program_id(0)
        for g in range(groups):
            part = jnp.dot(lhs_ref[...], mats[g][...], preferred_element_type=F32)

            @pl.when(step == 0)
            def _():
                acc_ref[g] = part

            @pl.when(step > 0)
            def _():
                acc_ref[g] += part

        @pl.when(step == steps - 1)
        def _():
            out_ref[...] = acc_ref[...].astype(BF16)

    return pl.pallas_call(
        body,
        grid=(steps,),
        out_shape=jax.ShapeDtypeStruct((groups, tokens, WIDTH), BF16),
        in_specs=[pl.BlockSpec((tokens, depth), lambda k: (0, k))]
        + [pl.BlockSpec((depth, WIDTH), lambda k, g=g: (k, group + g)) for g in range(groups)]
        + [ANY] * len(deps),
        out_specs=pl.BlockSpec((groups, tokens, WIDTH), lambda k: (0, 0, 0)),
        scratch_shapes=[pltpu.VMEM((groups, tokens, WIDTH), F32)],
        compiler_params=pltpu.CompilerParams(vmem_limit_bytes=VMEM_LIMIT),
        cost_estimate=COST,
        name="group_product",
    )(lhs, *[mat] * groups, *deps)


def squares(acts, deps):
    tokens, rows = acts.shape
    depth = largest_divisor(rows, 768, 128)

    def body(acts_ref, *rest):
        wide = acts_ref[...].astype(F32)
        rest[-1][...] = (wide * wide).astype(BF16).T

    return pl.pallas_call(
        body,
        grid=(rows // depth,),
        out_shape=jax.ShapeDtypeStruct((rows, tokens), BF16),
        in_specs=[pl.BlockSpec((tokens, depth), lambda k: (0, k))] + [ANY] * len(deps),
        out_specs=pl.BlockSpec((depth, tokens), lambda k: (k, 0)),
        compiler_params=pltpu.CompilerParams(vmem_limit_bytes=VMEM_LIMIT),
        cost_estimate=COST,
        name="squares",
    )(acts, *deps)


class Piece:
    def __init__(self, group, first, units, place):
        self.group, self.first, self.units, self.place = group, first, units, place


class Plan:
    def __init__(self, rows, cols):
        self.rows, self.cols = rows, cols
        self.half = rows // 2
        self.groups = cols // WIDTH
        self.unit = largest_divisor(self.half, UNIT_ROWS, 16)
        self.units = self.half // self.unit
        self.part_units = largest_divisor(self.units, MOST, 1)
        self.parts = self.units // self.part_units
        self.pieces = []
        for group in range(self.groups):
            first = 0
            while first < self.units:
                left = self.units - first
                units = min(self.part_units, left)
                if group == self.groups - 1:
                    units = max(min(units, LEAST), min(units, left // 3))
                units = min(units, self.part_units - first % self.part_units)
                self.pieces.append(Piece(group, first, units, len([p for p in self.pieces if p.group == group])))
                first += units

    def part_of(self, piece):
        return piece.first // self.part_units, piece.first % self.part_units


def cut(plan, tasks, deps):
    parts, tokens = plan.parts, tasks[0].shape[0]
    part = plan.half // parts
    unit = largest_divisor(part, 384, 128)
    halves = sum(task.shape[1] // plan.half for task in tasks)
    if unit % 128:
        wide = jnp.concatenate(tasks, axis=1).astype(F32)
        whole = (wide * wide).astype(BF16).T.reshape(halves, parts, part, tokens)
        return [whole[:, q] for q in range(parts)]
    ins, in_specs = [], []
    for task in tasks:
        for h in range(task.shape[1] // plan.half):
            for q in range(parts):
                ins.append(task)
                first = (h * parts + q) * (part // unit)
                in_specs.append(pl.BlockSpec((tokens, unit), lambda j, first=first: (0, first + j)))

    def body(*refs):
        for h in range(halves):
            for q in range(parts):
                wide = refs[h * parts + q][...].astype(F32)
                refs[len(refs) - parts + q][h] = (wide * wide).T.astype(BF16)

    return pl.pallas_call(
        body,
        grid=(part // unit,),
        out_shape=[jax.ShapeDtypeStruct((halves, part, tokens), BF16)] * parts,
        in_specs=in_specs + [ANY] * len(deps),
        out_specs=[pl.BlockSpec((halves, unit, tokens), lambda j: (0, j, 0))] * parts,
        compiler_params=pltpu.CompilerParams(vmem_limit_bytes=VMEM_LIMIT),
        cost_estimate=COST,
        name="cut",
    )(*ins, *deps)


def slot_call(plan, flags, last, fold=None, merge=None, gather=None, send=None, final=None, carry=None, cross=None, deps=()):
    unit = plan.unit
    ins, in_specs, outs, out_specs, aliases, kinds = [], [], [], [], {}, []
    most = lambda *some: max([part[0].units for part in some if part is not None] + [0])
    extra = lambda array: 0 if array is None else -(-array.shape[1] // unit)
    steps = max(
        most(final), most(gather, send) + extra(carry), most(fold, merge) + extra(cross)
    )

    def take(array, spec):
        ins.append(array)
        in_specs.append(spec)
        return len(ins) - 1

    def give(kind, shape, spec):
        outs.append(jax.ShapeDtypeStruct(shape, BF16))
        out_specs.append(spec)
        kinds.append(kind)
        return len(outs) - 1

    def at(piece, j):
        return jnp.minimum(j, piece.units - 1) if piece.units < steps else j

    def half_of(kind, flag):
        return {"sent": flag[0], "kept": 1 - flag[0]}.get(kind, kind)

    def rows_spec(piece, kind, width, column):
        return pl.BlockSpec(
            (unit, width),
            lambda j, flag: (half_of(kind, flag) * plan.units + piece.first + at(piece, j), column),
        )

    def half_spec(piece, kind):
        return pl.BlockSpec((None, unit, WIDTH), lambda j, flag: (half_of(kind, flag), at(piece, j), 0))

    def both_spec(piece):
        return pl.BlockSpec((2, unit, WIDTH), lambda j, flag: (0, at(piece, j), 0))

    def take_gsq(gsq, h):
        array, g = gsq
        shape = (array.shape[0], None, None) + array.shape[3:]
        return take(array, pl.BlockSpec(shape, lambda j, flag: (0, h, g, 0, 0)))

    def give_long(kind, count, units, tail):
        total = units + extra(tail)
        last_block = total - 1
        out = give(
            kind,
            (count, units * unit + (0 if tail is None else tail.shape[1]), WIDTH),
            pl.BlockSpec((count, unit, WIDTH), lambda j, flag: (0, jnp.minimum(j, last_block), 0)),
        )
        if tail is None:
            return out, None
        blocks = extra(tail) - 1
        spec = pl.BlockSpec((2, unit, WIDTH), lambda j, flag: (0, jnp.clip(j - units, 0, blocks), 0))
        return out, (take(tail, spec), units, total)

    def take_side(piece, kind, tasks):
        ids = []
        squared, gsq = tasks
        for h, asq in enumerate(squared):
            if isinstance(asq, list):
                q, offset = plan.part_of(piece)
                array = asq[q]
                spec = pl.BlockSpec(
                    (array.shape[0], None, unit, array.shape[3]),
                    lambda j, flag: (0, half_of(kind, flag), offset + at(piece, j), 0),
                )
            else:
                array, spec = asq, rows_spec(piece, kind, asq.shape[1], 0)
            ids.append((take(array, spec), take_gsq(gsq, h)))
        return ids

    def take_other(piece, tasks):
        parts, gsq = tasks
        q, offset = plan.part_of(piece)
        array = parts[q]
        return [
            (
                take(
                    array,
                    pl.BlockSpec(
                        (array.shape[0], None, unit, array.shape[3]),
                        lambda j, flag, h=h: (0, h, offset + at(piece, j), 0),
                    ),
                ),
                take_gsq(gsq, h),
            )
            for h in range(gsq[0].shape[1])
        ]

    if fold is not None:
        piece, weight, received, side = fold
        fold_w = take(weight, rows_spec(piece, "sent", WIDTH, piece.group))
        fold_in = take(received, half_spec(piece, "sent"))
        fold_side = take_side(piece, "sent", side)
    if merge is not None:
        piece, weight, received, side, mean, other = merge
        merge_w = take(weight, rows_spec(piece, "kept", WIDTH, piece.group))
        merge_in = take(received, half_spec(piece, "kept"))
        merge_side = take_side(piece, "kept", side)
        merge_mean = take(mean, half_spec(piece, 0))
        merge_other = take_other(piece, other)
    across = [part for part in (fold, merge) if part is not None]
    if across:
        sections = 1 if fold is None else 2
        across_out, across_tail = give_long("across", sections, most(fold, merge), cross)
    if gather is not None or send is not None:
        if gather is not None:
            piece, kept, came, slot = gather
            gather_kept, gather_came = take(kept, half_spec(piece, slot)), take(came, half_spec(piece, slot))
        if send is not None:
            piece, inward, own = send
            if own:
                send_in = [take(inward, rows_spec(piece, h, WIDTH, piece.group)) for h in (0, 1)]
            else:
                send_in = [take(inward, half_spec(piece, h)) for h in (0, 1)]
        pass_out, pass_tail = give_long("pass", 2, most(gather, send), carry)
    if final is not None:
        piece, own, came, buffer = final
        final_own, final_in = take(own, both_spec(piece)), take(came, both_spec(piece))
        first, group = piece.first, piece.group
        final_piece = piece
        final_out = give(
            "final",
            (2, plan.half, plan.cols),
            pl.BlockSpec((2, unit, WIDTH), lambda j, flag: (0, first + at(final_piece, j), group)),
        )
        if buffer is not None:
            aliases[1 + take(buffer, ANY)] = final_out
    for dep in deps:
        take(dep, ANY)

    def body(flag, *refs):
        inr, outr = refs[: len(ins)], refs[len(ins) :]
        j = pl.program_id(0)

        def during(part, extra=True):
            units = part[0].units
            if units < steps:
                return pl.when((j < units) & extra)
            return pl.when(extra) if extra is not True else (lambda f: f())

        def fisher(task):
            ref = inr[task[0]]
            if len(ref.shape) == 3:
                asq = jnp.concatenate([ref[b] for b in range(ref.shape[0])], axis=1)
            else:
                asq = ref[...]
            gsq = inr[task[1]][...]
            return jnp.dot(asq, gsq.reshape(-1, gsq.shape[-1]), preferred_element_type=F32)

        def summed(tasks):
            return functools.reduce(lambda a, b: a + b, [fisher(task) for task in tasks])

        def follow(out, tail):
            ref, start, stop = tail

            @pl.when((j >= start) & (j < stop))
            def _():
                outr[out][...] = inr[ref][...]

        if carry is not None:
            follow(pass_out, pass_tail)
        if cross is not None:
            follow(across_out, across_tail)
        if send is not None:

            @during(send, flag[1] != last)
            def _():
                for h in (0, 1):
                    outr[pass_out][h] = inr[send_in[h]][...]

        if gather is not None:

            @during(gather, flag[1] == last)
            def _():
                outr[pass_out][flag[0]] = inr[gather_came][...]
                outr[pass_out][1 - flag[0]] = inr[gather_kept][...]

        if final is not None:

            @during(final, flag[1] == last)
            def _():
                outr[final_out][...] = inr[final_own][...]

            @during(final, flag[1] != last)
            def _():
                outr[final_out][...] = inr[final_in][...]

        if fold is not None:

            @during(fold)
            def _():
                here, before = fisher(fold_side[0]), summed(fold_side[1:])
                total = here + before
                mean = (here * inr[fold_w][...].astype(F32) + before * inr[fold_in][...].astype(F32)) / total
                outr[across_out][0] = jnp.where(total > 0, mean, 0.0).astype(BF16)

        if merge is not None:

            @during(merge)
            def _():
                here, before, there = fisher(merge_side[0]), summed(merge_side[1:]), summed(merge_other)
                numer = (
                    here * inr[merge_w][...].astype(F32)
                    + before * inr[merge_in][...].astype(F32)
                    + there * inr[merge_mean][...].astype(F32)
                )
                outr[across_out][sections - 1] = (numer / (here + before + there + 1e-6)).astype(BF16)

    result = pl.pallas_call(
        body,
        grid_spec=pltpu.PrefetchScalarGridSpec(
            num_scalar_prefetch=1, grid=(steps,), in_specs=in_specs, out_specs=out_specs
        ),
        out_shape=outs,
        input_output_aliases=aliases,
        compiler_params=pltpu.CompilerParams(vmem_limit_bytes=VMEM_LIMIT),
        cost_estimate=COST,
        name="slot",
    )(flags, *ins)
    return dict(zip(kinds, result))


def local(sizes, activations, weights, labels, prototypes):
    tasks, rows_n, cols_n = sizes
    side_n = tasks // 2
    last = side_n - 1
    acts, weight, label_row, protos = activations[0], weights[0], labels[0], prototypes[0]
    block_tokens = acts.shape[0]
    tokens = block_tokens * cols_n
    share = tokens // rows_n
    plan = Plan(*weight.shape)
    place, row = lax.axis_index("task"), lax.axis_index("row")
    depth = jnp.minimum(place, tasks - 1 - place)
    sent = (place >= side_n).astype(jnp.int32)
    flags = jnp.stack([sent, depth.astype(jnp.int32)])

    mirrored = lambda pairs: pairs + [(tasks - 1 - a, tasks - 1 - b) for a, b in pairs]
    step_in = lambda d: mirrored([(d, d + 1)])
    step_out = lambda d: mirrored([(d + 1, d)])
    all_in = mirrored([(d, d + 1) for d in range(last)])
    send_in = lambda x: lax.ppermute(x, "task", all_in)
    send_mid = lambda x: lax.ppermute(x, "task", [(last, side_n), (side_n, last)])
    swap = lambda x: lax.ppermute(x, "task", step_in(last - 1) + step_out(last - 1))
    send_row = lambda x, s: lax.ppermute(x, "row", [(i, (i + s) % rows_n) for i in range(rows_n)])

    def sum_rows(full):
        cut_out = lambda r: lax.dynamic_slice_in_dim(full, r * share, share, 1)
        got = [send_row(cut_out((row + s) % rows_n), s) for s in range(1, rows_n)]
        total = cut_out(row).astype(F32)
        for part in got:
            total = total + part.astype(F32)
        return total

    def gather_rows(part):
        full = jnp.zeros((rows_n,) + part.shape, part.dtype)
        full = lax.dynamic_update_index_in_dim(full, part, row, 0)
        for s in range(1, rows_n):
            full = lax.dynamic_update_index_in_dim(full, send_row(part, s), (row - s) % rows_n, 0)
        return full

    full_acts = lax.all_gather(acts, "col", axis=0, tiled=True)

    near = [acts]
    for _ in range(last):
        near.append(send_in(near[-1]))
    cross = [send_mid(lax.dynamic_slice_in_dim(x, sent * plan.half, plan.half, 1)) for x in near]

    my_labels = lax.dynamic_slice_in_dim(label_row, row * share, share, 0)
    onehot = (my_labels[:, None] == lax.broadcasted_iota(jnp.int32, (share, protos.shape[0]), 1)).astype(BF16)
    target = jnp.dot(onehot, protos, preferred_element_type=F32)

    def squared_grad(product, group):
        groups = product.shape[0]
        wanted = target[:, group * WIDTH : (group + groups) * WIDTH].reshape(share, groups, WIDTH)
        grad = sum_rows(product) - jnp.moveaxis(wanted, 1, 0)
        return (grad * grad).astype(BF16)

    def packed(array):
        flat = array.reshape(-1, WIDTH)
        fill = -flat.shape[0] % 32
        return jnp.pad(flat, ((0, fill), (0, 0))).reshape(2, -1, WIDTH)

    def unpacked(array, shape):
        size = functools.reduce(lambda a, b: a * b, shape[:-1])
        rows = size + -size % 32
        return array[:, array.shape[1] - rows // 2 :].reshape(-1, WIDTH)[:size].reshape(shape)

    class Gradient:
        def __init__(self, group, groups):
            self.first, self.groups = group, groups
            self.outer, self.far = [None] * groups, [[None, None] for _ in range(groups)]

        def start(self, product):
            self.near = [squared_grad(product, self.first)]
            for _ in range(last - 1):
                self.near.append(send_in(self.near[-1]))

        def inwards(self, g):
            return packed(jnp.stack([x[g] for x in self.near]))

        def inside(self, g, came):
            self.outer[g] = unpacked(came, (last, share, WIDTH))
            if all(x is not None for x in self.outer):
                stacked = jnp.concatenate([self.near[0][None], jnp.stack(self.outer, 1)])
                self.own = gather_rows(stacked)

        def outside(self, g, part, came):
            self.far[g][part] = unpacked(came, (last if part else 1, share, WIDTH))
            if all(x is not None for pair in self.far for x in pair):
                self.oth = gather_rows(jnp.stack([jnp.concatenate(pair) for pair in self.far], 1))

    count = len(plan.pieces)
    batches = [Gradient(0, 1)]
    while batches[-1].first + batches[-1].groups < plan.groups:
        group = batches[-1].first + batches[-1].groups
        batches.append(Gradient(group, min(2, plan.groups - group)))
    batch_of = {b.first + g: b for b in batches for g in range(b.groups)}
    own_of = lambda piece: (batch_of[piece.group].own, piece.group - batch_of[piece.group].first)
    other_of = lambda piece: (batch_of[piece.group].oth, piece.group - batch_of[piece.group].first)

    def inward(index):
        piece = plan.pieces[index]
        if last == 1:
            return (piece, weight, True)
        a, b = piece.first * plan.unit, (piece.first + piece.units) * plan.unit
        q, offset = plan.part_of(piece)
        offset *= plan.unit
        columns = slice(piece.group * WIDTH, (piece.group + 1) * WIDTH)
        mine = weight.reshape(2, plan.half, plan.cols)[:, a:b, columns]
        squared = [own_square.reshape(2, plan.half, tokens)[:, a:b]]
        for task in outer_parts[: last - 1]:
            blocks = task[q][:, :, offset : offset + b - a]
            squared.append(jnp.moveaxis(blocks, 0, 2).reshape(2, b - a, tokens))
        own, g = own_of(piece)
        gsq = jnp.moveaxis(own[:, :, g], 0, 1).reshape(side_n, tokens, WIDTH)
        shares = [
            jnp.einsum("hrt,tc->hrc", s, g, preferred_element_type=F32)
            for s, g in zip(squared, gsq)
        ]
        mean, before = mine, jnp.zeros(mine.shape, F32)
        for d in range(1, last):
            came = lax.ppermute(mean, "task", step_in(d - 1)).astype(F32)
            before = before + shares[d]
            total = shares[0] + before
            value = (shares[0] * mine.astype(F32) + before * came) / total
            mean = jnp.where(depth == 0, mine, jnp.where(total > 0, value, 0.0).astype(BF16))
        return (piece, mean, False)

    def outward(came):
        for d in reversed(range(last - 1)):
            arrived = lax.ppermute(came, "task", step_out(d))
            came = jnp.where(depth == d, arrived, came)
        return came

    sent_pass, came_pass = {}, {}

    def start_pass(slot, got):
        if "pass" in got:
            sent_pass[slot] = got["pass"]
            came_pass[slot] = swap(got["pass"])

    if last == 1:
        start_pass(-2, slot_call(plan, flags, last, send=inward(0), deps=[near[-1], cross[0]]))
    lead = batches[0]
    product = group_product(full_acts, weight, 0, 1, deps=list(sent_pass.values()) + cross[1:])
    outer_cuts = [cut(plan, [task], [product]) for task in near[1:]]
    other_cuts = cut(plan, cross, [product])
    gather_col = lambda x: lax.all_gather(x, "col", axis=0)
    outer_parts = [[None] * plan.parts for _ in range(last)]
    other_parts = []
    for q in range(plan.parts):
        for h in range(last):
            outer_parts[h][q] = gather_col(outer_cuts[h][q])
        other_parts.append(gather_col(other_cuts[q]))

    def at_once(b, product):
        b.start(product)
        came = swap(jnp.stack(b.near))
        b.outer = [came[:, g] for g in range(b.groups)]
        stacked = jnp.concatenate([b.near[0][None], came])
        b.own = gather_rows(stacked)
        crossed = send_mid(stacked)
        b.oth = gather_rows(crossed)
        return crossed

    lead_far = at_once(lead, product)
    own_square = squares(full_acts, [lead.near[0], outer_cuts[0][0], other_cuts[0]])
    carries, crossings, starts = {}, {}, {}

    def ship(slot, b):
        for g in range(b.groups):
            carries[slot + g] = (b, g)
            crossings[slot + g] = (b, g, 0)
            crossings[slot + LAG + g] = (b, g, 1)

    if last == 1 and count > 1:
        start_pass(-1, slot_call(plan, flags, last, send=inward(1), deps=[own_square, lead.outer[0]]))
    product = own_square
    for b in batches[1:]:
        first = min(i for i, p in enumerate(plan.pieces) if p.group == b.first)
        ready = first - (0 if last == 1 else LAG) - LAG - (b.groups - 1)
        if ready >= 2:
            starts[ready - 2] = b
            continue
        deps = [product, lead.outer[0]] + list(sent_pass.values())[-1:]
        product = group_product(full_acts, weight, b.first, b.groups, deps=deps)
        if ready >= 0:
            b.start(product)
            ship(0, b)
        else:
            at_once(b, product)
    if last > 1:
        for index in range(min(LAG, count)):
            start_pass(index - LAG, slot_call(plan, flags, last, send=inward(index)))

    sent_mid, came_mid, places = {}, {}, {}
    buffer = None
    results, finished = [], 0
    chain = [product, lead_far] + list(sent_pass.values())[-1:]
    for slot in range(count + 3 * LAG):
        deps = list(chain)
        stage = {}
        now = lambda index: 0 <= index < count
        side_of = lambda piece: ([own_square] + outer_parts, own_of(piece))
        if slot - LAG in carries:
            b, g = carries[slot - LAG]
            b.inside(g, came_pass[slot - LAG])
        if slot - LAG in crossings:
            b, g, part = crossings[slot - LAG]
            b.outside(g, part, came_mid[slot - LAG])
        if slot in crossings:
            b, g, part = crossings[slot]
            stage["cross"] = packed(b.outer[g] if part else b.near[0][g])
        if slot in carries:
            b, g = carries[slot]
            stage["carry"] = b.inwards(g)
        if now(slot):
            piece = plan.pieces[slot]
            stage["fold"] = (piece, weight, came_pass[slot - LAG], side_of(piece))
        if now(slot + LAG):
            stage["send"] = inward(slot + LAG)
        index = slot - LAG
        if now(index):
            piece = plan.pieces[index]
            stage["merge"] = (
                piece,
                weight,
                came_pass[index - LAG],
                side_of(piece),
                came_mid[index],
                (other_parts, other_of(piece)),
            )
        index = slot - 2 * LAG
        if now(index):
            stage["gather"] = (plan.pieces[index], sent_mid[slot - LAG], came_mid[slot - LAG], places[slot - LAG])
        index = slot - 3 * LAG
        if now(index):
            stage["final"] = (
                plan.pieces[index],
                sent_pass[slot - LAG],
                outward(came_pass[slot - LAG]),
                buffer,
            )
        got = slot_call(plan, flags, last, deps=deps, **stage)
        chain = [got[name] for name in ("across", "pass") if name in got][:1]
        if "across" in got:
            sent_mid[slot], came_mid[slot] = got["across"], send_mid(got["across"])
            places[slot] = got["across"].shape[0] - 1
        start_pass(slot, got)
        if "final" in got:
            buffer = got["final"]
            done = plan.pieces[slot - 3 * LAG]
            stored = done.group + 1 - finished
            if done.first + done.units == plan.units and (stored == 2 or done.group == plan.groups - 1):
                whole = buffer.reshape(plan.rows, plan.cols)
                out = group_product(full_acts, whole, finished, stored)
                chain = [out]
                results.append(sum_rows(out).astype(BF16))
                finished = done.group + 1
        if slot in starts:
            b = starts[slot]
            product = group_product(full_acts, weight, b.first, b.groups, deps=chain)
            chain = [product]
            b.start(product)
            ship(slot + 1, b)
    result = jnp.moveaxis(jnp.concatenate(results), 0, 1).reshape(1, share, plan.cols)
    return buffer.reshape(plan.rows, plan.cols), result


def solution(mesh):
    placed = (
        P("task", "col", "row"),
        P("task", "row", "col"),
        P("task", None),
        P("task", None, "col"),
    )
    sizes = (mesh.shape["task"], mesh.shape["row"], mesh.shape["col"])
    return jax.shard_map(
        functools.partial(local, sizes),
        mesh=mesh,
        in_specs=placed,
        out_specs=(P("row", "col"), P("task", "row", "col")),
        check_vma=False,
    )
```

```python
import functools

import jax
import jax.numpy as jnp
from jax import lax
from jax.experimental import pallas as pl
from jax.experimental.pallas import tpu as pltpu
from jax.sharding import PartitionSpec as P

BF16 = jnp.bfloat16
F32 = jnp.float32
ANY = pl.BlockSpec(memory_space=pl.ANY)
WIDTH = 256
UNIT_ROWS = 384
MOST = 3
AHEAD = 3
LAG = 2
VMEM_LIMIT = 60 * 1024 * 1024
COST = pl.CostEstimate(flops=0, bytes_accessed=0, transcendentals=0)


def largest_divisor(total, limit, unit):
    best = total
    for size in range(unit, limit + 1, unit):
        if total % size == 0:
            best = size
    return best


def tie(arrays, deps):
    count = len(arrays)

    def body(*refs):
        pass

    return pl.pallas_call(
        body,
        out_shape=[jax.ShapeDtypeStruct(x.shape, x.dtype) for x in arrays],
        in_specs=[ANY] * (count + len(deps)),
        out_specs=[ANY] * count,
        input_output_aliases={i: i for i in range(count)},
        cost_estimate=COST,
        name="tie",
    )(*arrays, *deps)


def group_product(lhs, mat, group, groups, deps=()):
    tokens, rows = lhs.shape
    depth = largest_divisor(rows, 1152, 128)
    steps = rows // depth

    def body(lhs_ref, *rest):
        mats, (out_ref, acc_ref) = rest[:groups], rest[-2:]
        step = pl.program_id(0)
        for g in range(groups):
            part = jnp.dot(lhs_ref[...], mats[g][...], preferred_element_type=F32)

            @pl.when(step == 0)
            def _():
                acc_ref[g] = part

            @pl.when(step > 0)
            def _():
                acc_ref[g] += part

        @pl.when(step == steps - 1)
        def _():
            out_ref[...] = acc_ref[...].astype(BF16)

    return pl.pallas_call(
        body,
        grid=(steps,),
        out_shape=jax.ShapeDtypeStruct((groups, tokens, WIDTH), BF16),
        in_specs=[pl.BlockSpec((tokens, depth), lambda k: (0, k))]
        + [pl.BlockSpec((depth, WIDTH), lambda k, g=g: (k, group + g)) for g in range(groups)]
        + [ANY] * len(deps),
        out_specs=pl.BlockSpec((groups, tokens, WIDTH), lambda k: (0, 0, 0)),
        scratch_shapes=[pltpu.VMEM((groups, tokens, WIDTH), F32)],
        compiler_params=pltpu.CompilerParams(vmem_limit_bytes=VMEM_LIMIT),
        cost_estimate=COST,
        name="group_product",
    )(lhs, *[mat] * groups, *deps)


def squares(acts, deps):
    tokens, rows = acts.shape
    depth = largest_divisor(rows, 768, 128)

    def body(acts_ref, *rest):
        wide = acts_ref[...].astype(F32)
        rest[-1][...] = (wide * wide).astype(BF16).T

    return pl.pallas_call(
        body,
        grid=(rows // depth,),
        out_shape=jax.ShapeDtypeStruct((rows, tokens), BF16),
        in_specs=[pl.BlockSpec((tokens, depth), lambda k: (0, k))] + [ANY] * len(deps),
        out_specs=pl.BlockSpec((depth, tokens), lambda k: (k, 0)),
        compiler_params=pltpu.CompilerParams(vmem_limit_bytes=VMEM_LIMIT),
        cost_estimate=COST,
        name="squares",
    )(acts, *deps)


class Piece:
    def __init__(self, group, first, units, place):
        self.group, self.first, self.units, self.place = group, first, units, place


class Plan:
    def __init__(self, rows, cols):
        self.rows, self.cols = rows, cols
        self.half = rows // 2
        self.groups = cols // WIDTH
        self.unit = largest_divisor(self.half, UNIT_ROWS, 16)
        self.units = self.half // self.unit
        lead = largest_divisor(self.units, MOST, 1)
        self.bounds = [(0, self.units)]
        self.pieces = []
        for group in range(self.groups):
            first = 0
            while first < self.units:
                left = self.units - first
                units = min(lead, left)
                self.pieces.append(Piece(group, first, units, len([p for p in self.pieces if p.group == group])))
                first += units

    def part_of(self, piece):
        q = [a <= piece.first < b for a, b in self.bounds].index(True)
        return q, piece.first - self.bounds[q][0]


def cut(plan, tasks, deps):
    unit, tokens = plan.unit, tasks[0].shape[0]
    parts = [b - a for a, b in plan.bounds]
    halves = sum(task.shape[1] // plan.half for task in tasks)
    steps = MOST
    if unit % 128 or any(part % steps for part in parts):
        wide = jnp.concatenate(tasks, axis=1).astype(F32)
        whole = (wide * wide).astype(BF16).T.reshape(halves, plan.half, tokens)
        return [whole[:, a * unit : b * unit] for a, b in plan.bounds]
    ins, in_specs, places = [], [], []
    count = 0
    for task in tasks:
        for h in range(task.shape[1] // plan.half):
            for q, (a, b) in enumerate(plan.bounds):
                per = (b - a) // steps
                for i in range(per):
                    first = h * plan.units + a + i
                    ins.append(task)
                    in_specs.append(
                        pl.BlockSpec((tokens, unit), lambda j, first=first, per=per: (0, first + per * j))
                    )
                    places.append((q, count, i))
            count += 1

    def body(*refs):
        outs = refs[len(refs) - len(parts) :]
        for ref, (q, h, i) in zip(refs, places):
            wide = ref[...].astype(F32)
            outs[q][h, i * unit : (i + 1) * unit] = (wide * wide).T.astype(BF16)

    return pl.pallas_call(
        body,
        grid=(steps,),
        out_shape=[jax.ShapeDtypeStruct((halves, part * unit, tokens), BF16) for part in parts],
        in_specs=in_specs + [ANY] * len(deps),
        out_specs=[
            pl.BlockSpec((halves, part // steps * unit, tokens), lambda j: (0, j, 0)) for part in parts
        ],
        compiler_params=pltpu.CompilerParams(vmem_limit_bytes=VMEM_LIMIT),
        cost_estimate=COST,
        name="cut",
    )(*ins, *deps)


def slot_call(plan, flags, last, fold=None, merge=None, gather=None, send=None, final=None, ahead=None, carry=None, cross=None, deps=()):
    unit = plan.unit
    ins, in_specs, outs, out_specs, aliases, kinds = [], [], [], [], {}, []
    most = lambda *some: max([part[0].units for part in some if part is not None] + [0])
    extra = lambda array: 0 if array is None else -(-array.shape[1] // unit)
    steps = max(
        most(final), most(merge, gather, send) + extra(carry), most(fold, merge) + extra(cross), 0 if ahead is None else AHEAD
    )

    def take(array, spec):
        ins.append(array)
        in_specs.append(spec)
        return len(ins) - 1

    def give(kind, shape, spec, dtype=BF16):
        outs.append(jax.ShapeDtypeStruct(shape, dtype))
        out_specs.append(spec)
        kinds.append(kind)
        return len(outs) - 1

    def at(piece, j):
        return jnp.minimum(j, piece.units - 1) if piece.units < steps else j

    def half_of(kind, flag):
        return {"sent": flag[0], "kept": 1 - flag[0]}.get(kind, kind)

    def rows_spec(piece, kind, width, column):
        return pl.BlockSpec(
            (unit, width),
            lambda j, flag: (half_of(kind, flag) * plan.units + piece.first + at(piece, j), column),
        )

    def half_spec(piece, kind):
        return pl.BlockSpec((None, unit, WIDTH), lambda j, flag: (half_of(kind, flag), at(piece, j), 0))

    def take_gsq(gsq, h):
        shape = (gsq.shape[0], None) + gsq.shape[2:]
        return take(gsq, pl.BlockSpec(shape, lambda j, flag: (0, h, 0, 0)))

    def give_long(kind, count, units, tail):
        total = units + extra(tail)
        last_block = total - 1
        out = give(
            kind,
            (count, units * unit + (0 if tail is None else tail.shape[1]), WIDTH),
            pl.BlockSpec((count, unit, WIDTH), lambda j, flag: (0, jnp.minimum(j, last_block), 0)),
        )
        if tail is None:
            return out, None
        blocks = extra(tail) - 1
        spec = pl.BlockSpec((2, unit, WIDTH), lambda j, flag: (0, jnp.clip(j - units, 0, blocks), 0))
        return out, (take(tail, spec), units, total)

    def take_side(piece, kind, tasks):
        ids = []
        squared, gsq = tasks
        for h, asq in enumerate(squared):
            if isinstance(asq, list):
                q, offset = plan.part_of(piece)
                array = asq[q]
                spec = pl.BlockSpec(
                    (array.shape[0], None, unit, array.shape[3]),
                    lambda j, flag: (0, half_of(kind, flag), offset + at(piece, j), 0),
                )
            else:
                array, spec = asq, rows_spec(piece, kind, asq.shape[1], 0)
            ids.append((take(array, spec), take_gsq(gsq, h)))
        return ids

    def take_other(piece, tasks):
        parts, gsq = tasks
        q, offset = plan.part_of(piece)
        array = parts[q]
        return [
            (
                take(
                    array,
                    pl.BlockSpec(
                        (array.shape[0], None, unit, array.shape[3]),
                        lambda j, flag, h=h: (0, h, offset + at(piece, j), 0),
                    ),
                ),
                take_gsq(gsq, h),
            )
            for h in range(gsq.shape[1])
        ]

    if fold is not None:
        piece, weight, received, side = fold
        fold_w = take(weight, rows_spec(piece, "sent", WIDTH, piece.group))
        fold_in = take(received, half_spec(piece, "sent"))
        fold_side = take_side(piece, "sent", side)
    if merge is not None:
        piece, weight, received, side, mean, other = merge
        merge_w = take(weight, rows_spec(piece, "kept", WIDTH, piece.group))
        merge_in = take(received, half_spec(piece, "kept"))
        merge_side = take_side(piece, "kept", side)
        merge_mean = take(mean, half_spec(piece, 0))
        merge_other = take_other(piece, other)
    apart = fold is not None and merge is not None and fold[0].units != merge[0].units
    if fold is not None or merge is not None:
        sections = 1 if fold is None or apart else 2
        across_out, across_tail = give_long("across", sections, most(merge if fold is None else fold), cross)
        back_out, back_place = across_out, sections - 1
        if apart:
            back_out, back_place = give_long("back", 1, most(merge), None)[0], 0
    outgoing = [part for part in (merge, gather) if part is not None]
    if outgoing or send is not None:
        if gather is not None:
            piece, came, section = gather
            gather_came = take(came, half_spec(piece, section))
        if send is not None:
            piece, inward, own = send
            if own:
                send_in = [take(inward, rows_spec(piece, h, WIDTH, piece.group)) for h in (0, 1)]
            else:
                send_in = [take(inward, half_spec(piece, h)) for h in (0, 1)]
        pass_count = 2 if send is not None or merge is not None else 1
        pass_out, pass_tail = give_long("pass", pass_count, most(merge, gather, send), carry)
    if final is not None:
        piece, kept, crossed, buffer, acts, total = final
        final_kept = [take(x, half_spec(piece, kept[2])) for x in kept[:2]]
        final_crossed = [take(x, half_spec(piece, crossed[2])) for x in crossed[:2]]
        first, group = piece.first, piece.group
        final_piece = piece
        final_out = give(
            "final",
            (2, plan.half, plan.cols),
            pl.BlockSpec((2, unit, WIDTH), lambda j, flag: (0, first + at(final_piece, j), group)),
        )
        if buffer is not None:
            aliases[1 + take(buffer, ANY)] = final_out
        if acts is not None:
            result_acts = [
                take(
                    acts,
                    pl.BlockSpec(
                        (acts.shape[0], unit),
                        lambda j, flag, h=h: (0, h * plan.units + first + at(final_piece, j)),
                    ),
                )
                for h in (0, 1)
            ]
            whole = pl.BlockSpec((acts.shape[0], WIDTH), lambda j, flag: (0, 0))
            result_in = None if total is None else take(total, whole)
            result_out = give("result", (acts.shape[0], WIDTH), whole, F32)
    if ahead is not None:
        ahead_acts, ahead_weight, ahead_group, ahead_turn, ahead_total = ahead
        tokens, depth = ahead_acts.shape[0], plan.rows // AHEAD**2
        block_at = lambda j: ahead_turn * AHEAD + jnp.minimum(j, AHEAD - 1)
        ahead_lhs = take(ahead_acts, pl.BlockSpec((tokens, depth), lambda j, flag: (0, block_at(j))))
        ahead_mat = take(ahead_weight, pl.BlockSpec((depth, WIDTH), lambda j, flag: (block_at(j), ahead_group)))
        everything = pl.BlockSpec((tokens, WIDTH), lambda j, flag: (0, 0))
        ahead_in = None if ahead_total is None else take(ahead_total, everything)
        ahead_out = give("ahead", (tokens, WIDTH), everything, F32)
    for dep in deps:
        take(dep, ANY)

    def body(flag, *refs):
        inr, outr = refs[: len(ins)], refs[len(ins) :]
        j = pl.program_id(0)

        def during(part, extra=True):
            units = part[0].units
            if units < steps:
                return pl.when((j < units) & extra)
            return pl.when(extra) if extra is not True else (lambda f: f())

        def fisher(task):
            ref = inr[task[0]]
            if len(ref.shape) == 3:
                asq = jnp.concatenate([ref[b] for b in range(ref.shape[0])], axis=1)
            else:
                asq = ref[...]
            gsq = inr[task[1]][...]
            return jnp.dot(asq, gsq.reshape(-1, gsq.shape[-1]), preferred_element_type=F32)

        def summed(tasks):
            return functools.reduce(lambda a, b: a + b, [fisher(task) for task in tasks])

        def follow(out, tail):
            ref, start, stop = tail

            @pl.when((j >= start) & (j < stop))
            def _():
                outr[out][...] = inr[ref][...]

        if carry is not None:
            follow(pass_out, pass_tail)
        if cross is not None:
            follow(across_out, across_tail)
        if send is not None:

            @during(send, flag[1] != last)
            def _():
                for h in (0, 1):
                    outr[pass_out][h] = inr[send_in[h]][...]

        if gather is not None:

            @during(gather, flag[1] == last)
            def _():
                outr[pass_out][pass_count - 1] = inr[gather_came][...]

        if final is not None:

            @during(final, flag[1] == last)
            def _():
                outr[final_out][1 - flag[0]] = inr[final_kept[0]][...]
                outr[final_out][flag[0]] = inr[final_crossed[0]][...]

            @during(final, flag[1] != last)
            def _():
                outr[final_out][1 - flag[0]] = inr[final_kept[1]][...]
                outr[final_out][flag[0]] = inr[final_crossed[1]][...]

        def add_to(out, before, value):
            @pl.when(j == 0)
            def _():
                outr[out][...] = value if before is None else inr[before][...] + value

            @pl.when(j > 0)
            def _():
                outr[out][...] += value

        if final is not None and final[4] is not None:

            @during(final)
            def _():
                parts = [
                    jnp.dot(inr[result_acts[h]][...], outr[final_out][h], preferred_element_type=F32)
                    for h in (0, 1)
                ]
                add_to(result_out, result_in, parts[0] + parts[1])

        if ahead is not None:

            @pl.when(j < AHEAD)
            def _():
                add_to(
                    ahead_out,
                    ahead_in,
                    jnp.dot(inr[ahead_lhs][...], inr[ahead_mat][...], preferred_element_type=F32),
                )

        if fold is not None:

            @during(fold)
            def _():
                here, before = fisher(fold_side[0]), summed(fold_side[1:])
                total = here + before
                mean = (here * inr[fold_w][...].astype(F32) + before * inr[fold_in][...].astype(F32)) / total
                outr[across_out][0] = jnp.where(total > 0, mean, 0.0).astype(BF16)

        if merge is not None:

            @during(merge)
            def _():
                here, before, there = fisher(merge_side[0]), summed(merge_side[1:]), summed(merge_other)
                numer = (
                    here * inr[merge_w][...].astype(F32)
                    + before * inr[merge_in][...].astype(F32)
                    + there * inr[merge_mean][...].astype(F32)
                )
                value = (numer / (here + before + there + 1e-6)).astype(BF16)
                outr[back_out][back_place] = value

                @pl.when(flag[1] == last)
                def _():
                    outr[pass_out][0] = value

    result = pl.pallas_call(
        body,
        grid_spec=pltpu.PrefetchScalarGridSpec(
            num_scalar_prefetch=1, grid=(steps,), in_specs=in_specs, out_specs=out_specs
        ),
        out_shape=outs,
        input_output_aliases=aliases,
        compiler_params=pltpu.CompilerParams(vmem_limit_bytes=VMEM_LIMIT),
        cost_estimate=COST,
        name="slot",
    )(flags, *ins)
    return dict(zip(kinds, result))


def local(sizes, activations, weights, labels, prototypes):
    tasks, rows_n, cols_n = sizes
    side_n = tasks // 2
    last = side_n - 1
    acts, weight, label_row, protos = activations[0], weights[0], labels[0], prototypes[0]
    block_tokens = acts.shape[0]
    tokens = block_tokens * cols_n
    share = tokens // rows_n
    plan = Plan(*weight.shape)
    place, row = lax.axis_index("task"), lax.axis_index("row")
    depth = jnp.minimum(place, tasks - 1 - place)
    sent = (place >= side_n).astype(jnp.int32)
    flags = jnp.stack([sent, depth.astype(jnp.int32)])

    mirrored = lambda pairs: pairs + [(tasks - 1 - a, tasks - 1 - b) for a, b in pairs]
    step_in = lambda d: mirrored([(d, d + 1)])
    step_out = lambda d: mirrored([(d + 1, d)])
    all_in = mirrored([(d, d + 1) for d in range(last)])
    send_in = lambda x: lax.ppermute(x, "task", all_in)
    send_mid = lambda x: lax.ppermute(x, "task", [(last, side_n), (side_n, last)])
    swap = lambda x: lax.ppermute(x, "task", step_in(last - 1) + step_out(last - 1))
    send_row = lambda x, s: lax.ppermute(x, "row", [(i, (i + s) % rows_n) for i in range(rows_n)])

    def sum_rows(full):
        cut_out = lambda r: lax.dynamic_slice_in_dim(full, r * share, share, 1)
        got = [send_row(cut_out((row + s) % rows_n), s) for s in range(1, rows_n)]
        total = cut_out(row).astype(F32)
        for part in got:
            total = total + part.astype(F32)
        return total

    def gather_rows(part):
        full = jnp.zeros((rows_n,) + part.shape, part.dtype)
        full = lax.dynamic_update_index_in_dim(full, part, row, 0)
        for s in range(1, rows_n):
            full = lax.dynamic_update_index_in_dim(full, send_row(part, s), (row - s) % rows_n, 0)
        return full

    full_acts = lax.all_gather(acts, "col", axis=0, tiled=True)

    crossing = lambda x: send_mid(lax.dynamic_slice_in_dim(x, sent * plan.half, plan.half, 1))
    near, cross = [acts], [crossing(acts)]
    for _ in range(last):
        near += tie([send_in(near[-1])], cross[-1:])
        cross.append(crossing(near[-1]))

    my_labels = lax.dynamic_slice_in_dim(label_row, row * share, share, 0)
    onehot = (my_labels[:, None] == lax.broadcasted_iota(jnp.int32, (share, protos.shape[0]), 1)).astype(BF16)
    target = jnp.dot(onehot, protos, preferred_element_type=F32)

    def squared_grad(product, group):
        groups = product.shape[0]
        wanted = target[:, group * WIDTH : (group + groups) * WIDTH].reshape(share, groups, WIDTH)
        grad = sum_rows(product) - jnp.moveaxis(wanted, 1, 0)
        return (grad * grad).astype(BF16)

    def packed(array):
        flat = array.reshape(-1, WIDTH)
        fill = -flat.shape[0] % 32
        return jnp.pad(flat, ((0, fill), (0, 0))).reshape(2, -1, WIDTH)

    def unpacked(array, shape):
        size = functools.reduce(lambda a, b: a * b, shape[:-1])
        rows = size + -size % 32
        return array[:, array.shape[1] - rows // 2 :].reshape(-1, WIDTH)[:size].reshape(shape)

    class Gradient:
        def __init__(self, group, groups):
            self.first, self.groups = group, groups
            self.outer, self.own, self.far, self.oth = ([None] * groups for _ in range(4))

        def start(self, product):
            self.near = [squared_grad(product, self.first)]
            for _ in range(last - 1):
                self.near.append(send_in(self.near[-1]))

        def inwards(self, g):
            return packed(jnp.stack([x[g] for x in self.near]))

        def inside(self, g, came):
            self.outer[g] = unpacked(came, (last, share, WIDTH))
            self.own[g] = gather_rows(jnp.concatenate([self.near[0][g][None], self.outer[g]]))

        def outside(self, g, part, came):
            came = unpacked(came, (last if part else 1, share, WIDTH))
            if part:
                self.oth[g] = gather_rows(jnp.concatenate([self.far[g], came]))
            else:
                self.far[g] = came

    count = len(plan.pieces)
    batches = [Gradient(0, 1)]
    while batches[-1].first + batches[-1].groups < plan.groups:
        group = batches[-1].first + batches[-1].groups
        batches.append(Gradient(group, 1))
    batch_of = {b.first + g: b for b in batches for g in range(b.groups)}
    own_of = lambda piece: batch_of[piece.group].own[piece.group - batch_of[piece.group].first]
    other_of = lambda piece: batch_of[piece.group].oth[piece.group - batch_of[piece.group].first]

    def inward(index):
        piece = plan.pieces[index]
        if last == 1:
            return (piece, weight, True)
        a, b = piece.first * plan.unit, (piece.first + piece.units) * plan.unit
        q, offset = plan.part_of(piece)
        offset *= plan.unit
        columns = slice(piece.group * WIDTH, (piece.group + 1) * WIDTH)
        mine = weight.reshape(2, plan.half, plan.cols)[:, a:b, columns]
        squared = [own_square.reshape(2, plan.half, tokens)[:, a:b]]
        for task in outer_parts[: last - 1]:
            blocks = task[q][:, :, offset : offset + b - a]
            squared.append(jnp.moveaxis(blocks, 0, 2).reshape(2, b - a, tokens))
        gsq = jnp.moveaxis(own_of(piece), 0, 1).reshape(side_n, tokens, WIDTH)
        shares = [
            jnp.einsum("hrt,tc->hrc", s, g, preferred_element_type=F32)
            for s, g in zip(squared, gsq)
        ]
        mean, before = mine, jnp.zeros(mine.shape, F32)
        for d in range(1, last):
            came = lax.ppermute(mean, "task", step_in(d - 1)).astype(F32)
            before = before + shares[d]
            total = shares[0] + before
            value = (shares[0] * mine.astype(F32) + before * came) / total
            mean = jnp.where(depth == 0, mine, jnp.where(total > 0, value, 0.0).astype(BF16))
        return (piece, mean, False)

    def outward(came):
        for d in reversed(range(last - 1)):
            arrived = lax.ppermute(came, "task", step_out(d))
            came = jnp.where(depth == d, arrived, came)
        return came

    sent_pass, came_pass, came_out = {}, {}, {}

    def start_pass(slot, got):
        if "pass" in got:
            sent_pass[slot] = got["pass"]
            came_pass[slot] = swap(got["pass"])
            came_out[slot] = outward(came_pass[slot])

    if last == 1:
        start_pass(-2, slot_call(plan, flags, last, send=inward(0), deps=[near[-1], cross[0]]))
    lead = batches[0]
    outer_cuts = [cut(plan, [task], list(sent_pass.values())) for task in near[1:]]
    product = group_product(full_acts, weight, 0, 1, deps=[x[0] for x in outer_cuts])
    gather_col = lambda x: lax.all_gather(x, "col", axis=0)
    outer_parts = [[gather_col(x) for x in task] for task in outer_cuts]

    def at_once(b, product):
        b.start(product)
        came = swap(jnp.stack(b.near))
        b.outer = [came[:, g] for g in range(b.groups)]
        stacked = jnp.concatenate([b.near[0][None], came])
        crossed = send_mid(stacked)
        b.own = [gather_rows(stacked[:, g]) for g in range(b.groups)]
        b.oth = [gather_rows(crossed[:, g]) for g in range(b.groups)]
        return crossed

    lead_far = at_once(lead, product)
    own_square = squares(full_acts, [lead.near[0]] + list(came_pass.values()))
    carries, crossings, starts = {}, {}, {}

    def ship(slot, b):
        for g in range(b.groups):
            carries[slot + g] = (b, g)
            crossings[slot + g] = (b, g, 0)
            crossings[slot + LAG + g] = (b, g, 1)

    if last == 1 and count > 1:
        start_pass(-1, slot_call(plan, flags, last, send=inward(1), deps=[lead.near[0]] + list(came_pass.values())))
    other_cuts = cut(plan, cross, [own_square] + list(sent_pass.values())[-1:])
    other_parts = [gather_col(x) for x in other_cuts]
    early = min(LAG, plan.groups - 1) if last == 1 else plan.groups - 1
    deps = [other_cuts[0], lead.outer[0]] + list(sent_pass.values())[-1:]
    next_products = group_product(full_acts, weight, 1, early, deps=deps)
    fused = last == 1 and plan.unit % 128 == 0 and plan.rows % (AHEAD**2 * 128) == 0
    first_of = lambda b: min(i for i, p in enumerate(plan.pieces) if p.group == b.first)
    rest = list(batches[1:])
    if fused and all(first_of(b) >= AHEAD * (i + 1) for i, b in enumerate(rest)):
        for slot, b in enumerate(rest[:LAG]):
            b.start(next_products[slot : slot + 1])
            ship(slot, b)
        turn = 0
        for b in rest[LAG:]:
            starts.update({turn + k: (b, k) for k in range(AHEAD)})
            turn += AHEAD
            slot = turn
            while {slot, slot + LAG} & set(crossings):
                slot += 1
            ship(slot, b)
    else:
        for i, b in enumerate(rest):
            at_once(b, next_products[i : i + 1])
    if last > 1:
        for index in range(min(LAG, count)):
            start_pass(index - LAG, slot_call(plan, flags, last, send=inward(index)))

    came_mid, backs = {}, {}
    buffer = None
    results = []
    chain = [next_products, lead_far] + list(came_pass.values())[-1:]
    ahead_total, result_total = None, None
    for slot in range(count + 3 * LAG):
        deps = list(chain)
        stage = {}
        now = lambda index: 0 <= index < count
        side_of = lambda piece: ([own_square] + outer_parts, own_of(piece))
        if slot - LAG in carries:
            b, g = carries[slot - LAG]
            b.inside(g, came_pass[slot - LAG])
        if slot - LAG in crossings:
            b, g, part = crossings[slot - LAG]
            b.outside(g, part, came_mid[slot - LAG])
        if slot in crossings:
            b, g, part = crossings[slot]
            stage["cross"] = packed(b.outer[g] if part else b.near[0][g])
        if slot in carries:
            b, g = carries[slot]
            stage["carry"] = b.inwards(g)
        if now(slot):
            piece = plan.pieces[slot]
            stage["fold"] = (piece, weight, came_pass[slot - LAG], side_of(piece))
        if now(slot + LAG):
            stage["send"] = inward(slot + LAG)
        if slot < max(carries, default=0):
            stage.setdefault("cross", packed(lead.near[0][0]))
            stage.setdefault("carry", lead.inwards(0))
        index = slot - LAG
        if now(index):
            piece = plan.pieces[index]
            stage["merge"] = (
                piece,
                weight,
                came_pass[index - LAG],
                side_of(piece),
                came_mid[index],
                (other_parts, other_of(piece)),
            )
        index = slot - 2 * LAG
        if now(index):
            stage["gather"] = (plan.pieces[index],) + backs[slot - LAG]
        index = slot - 3 * LAG
        if now(index):
            stage["final"] = (
                plan.pieces[index],
                (sent_pass[slot - 2 * LAG], came_out[slot - 2 * LAG], 0),
                (sent_pass[slot - LAG], came_out[slot - LAG], sent_pass[slot - LAG].shape[0] - 1),
                buffer,
                full_acts if fused else None,
                result_total,
            )
        if slot in starts:
            b, turn = starts[slot]
            stage["ahead"] = (full_acts, weight, b.first, turn, ahead_total)
        got = slot_call(plan, flags, last, deps=deps, **stage)
        chain = [got[name] for name in ("across", "pass") if name in got][:1]
        if "across" in got:
            came_mid[slot] = send_mid(got["across"])
            backs[slot] = (came_mid[slot], got["across"].shape[0] - 1)
            if "back" in got:
                backs[slot] = (send_mid(got["back"]), 0)
        start_pass(slot, got)
        if "final" in got:
            buffer = got["final"]
            done = plan.pieces[slot - 3 * LAG]
            result_total = got.get("result")
            if done.first + done.units == plan.units:
                if fused:
                    out = result_total.astype(BF16)[None]
                else:
                    out = group_product(full_acts, buffer.reshape(plan.rows, plan.cols), done.group, 1)
                results.append(sum_rows(out).astype(BF16))
                result_total = None
        if "ahead" in got:
            ahead_total = got["ahead"]
            b, turn = starts[slot]
            if turn == AHEAD - 1:
                b.start(ahead_total.astype(BF16)[None])
                ahead_total = None
    result = jnp.moveaxis(jnp.concatenate(results), 0, 1).reshape(1, share, plan.cols)
    return buffer.reshape(plan.rows, plan.cols), result


def solution(mesh):
    placed = (
        P("task", "col", "row"),
        P("task", "row", "col"),
        P("task", None),
        P("task", None, "col"),
    )
    sizes = (mesh.shape["task"], mesh.shape["row"], mesh.shape["col"])
    return jax.shard_map(
        functools.partial(local, sizes),
        mesh=mesh,
        in_specs=placed,
        out_specs=(P("row", "col"), P("task", "row", "col")),
        check_vma=False,
    )
```

```python
import functools

import jax
import jax.numpy as jnp
from jax import lax
from jax.experimental import pallas as pl
from jax.experimental.pallas import tpu as pltpu
from jax.sharding import PartitionSpec as P

BF16 = jnp.bfloat16
F32 = jnp.float32
ANY = pl.BlockSpec(memory_space=pl.ANY)
WIDTH = 256
UNIT_ROWS = 384
MOST = 3
AHEAD = 3
LAG = 2
VMEM_LIMIT = 60 * 1024 * 1024
COST = pl.CostEstimate(flops=0, bytes_accessed=0, transcendentals=0)


def largest_divisor(total, limit, unit):
    best = total
    for size in range(unit, limit + 1, unit):
        if total % size == 0:
            best = size
    return best


def tie(arrays, deps):
    count = len(arrays)

    def body(*refs):
        pass

    return pl.pallas_call(
        body,
        out_shape=[jax.ShapeDtypeStruct(x.shape, x.dtype) for x in arrays],
        in_specs=[ANY] * (count + len(deps)),
        out_specs=[ANY] * count,
        input_output_aliases={i: i for i in range(count)},
        cost_estimate=COST,
        name="tie",
    )(*arrays, *deps)


def group_product(lhs, mat, group, groups, deps=()):
    tokens, rows = lhs.shape
    depth = largest_divisor(rows, 1152, 128)
    steps = rows // depth

    def body(lhs_ref, *rest):
        mats, (out_ref, acc_ref) = rest[:groups], rest[-2:]
        step = pl.program_id(0)
        for g in range(groups):
            part = jnp.dot(lhs_ref[...], mats[g][...], preferred_element_type=F32)

            @pl.when(step == 0)
            def _():
                acc_ref[g] = part

            @pl.when(step > 0)
            def _():
                acc_ref[g] += part

        @pl.when(step == steps - 1)
        def _():
            out_ref[...] = acc_ref[...].astype(BF16)

    return pl.pallas_call(
        body,
        grid=(steps,),
        out_shape=jax.ShapeDtypeStruct((groups, tokens, WIDTH), BF16),
        in_specs=[pl.BlockSpec((tokens, depth), lambda k: (0, k))]
        + [pl.BlockSpec((depth, WIDTH), lambda k, g=g: (k, group + g)) for g in range(groups)]
        + [ANY] * len(deps),
        out_specs=pl.BlockSpec((groups, tokens, WIDTH), lambda k: (0, 0, 0)),
        scratch_shapes=[pltpu.VMEM((groups, tokens, WIDTH), F32)],
        compiler_params=pltpu.CompilerParams(vmem_limit_bytes=VMEM_LIMIT),
        cost_estimate=COST,
        name="group_product",
    )(lhs, *[mat] * groups, *deps)


def squares(acts, deps):
    tokens, rows = acts.shape
    depth = largest_divisor(rows, 768, 128)

    def body(acts_ref, *rest):
        wide = acts_ref[...].astype(F32)
        rest[-1][...] = (wide * wide).astype(BF16).T

    return pl.pallas_call(
        body,
        grid=(rows // depth,),
        out_shape=jax.ShapeDtypeStruct((rows, tokens), BF16),
        in_specs=[pl.BlockSpec((tokens, depth), lambda k: (0, k))] + [ANY] * len(deps),
        out_specs=pl.BlockSpec((depth, tokens), lambda k: (k, 0)),
        compiler_params=pltpu.CompilerParams(vmem_limit_bytes=VMEM_LIMIT),
        cost_estimate=COST,
        name="squares",
    )(acts, *deps)


class Piece:
    def __init__(self, group, first, units, place):
        self.group, self.first, self.units, self.place = group, first, units, place


class Plan:
    def __init__(self, rows, cols):
        self.rows, self.cols = rows, cols
        self.half = rows // 2
        self.groups = cols // WIDTH
        self.unit = largest_divisor(self.half, UNIT_ROWS, 16)
        self.units = self.half // self.unit
        lead = largest_divisor(self.units, MOST, 1)
        self.bounds = [(0, self.units)]
        self.pieces = []
        for group in range(self.groups):
            first = 0
            while first < self.units:
                left = self.units - first
                units = min(lead, left)
                self.pieces.append(Piece(group, first, units, len([p for p in self.pieces if p.group == group])))
                first += units

    def part_of(self, piece):
        q = [a <= piece.first < b for a, b in self.bounds].index(True)
        return q, piece.first - self.bounds[q][0]


def cut(plan, tasks, deps):
    unit, tokens = plan.unit, tasks[0].shape[0]
    parts = [b - a for a, b in plan.bounds]
    halves = sum(task.shape[1] // plan.half for task in tasks)
    steps = MOST
    if unit % 128 or any(part % steps for part in parts):
        wide = jnp.concatenate(tasks, axis=1).astype(F32)
        whole = (wide * wide).astype(BF16).T.reshape(halves, plan.half, tokens)
        return [whole[:, a * unit : b * unit] for a, b in plan.bounds]
    ins, in_specs, places = [], [], []
    count = 0
    for task in tasks:
        for h in range(task.shape[1] // plan.half):
            for q, (a, b) in enumerate(plan.bounds):
                per = (b - a) // steps
                for i in range(per):
                    first = h * plan.units + a + i
                    ins.append(task)
                    in_specs.append(
                        pl.BlockSpec((tokens, unit), lambda j, first=first, per=per: (0, first + per * j))
                    )
                    places.append((q, count, i))
            count += 1

    def body(*refs):
        outs = refs[len(refs) - len(parts) :]
        for ref, (q, h, i) in zip(refs, places):
            wide = ref[...].astype(F32)
            outs[q][h, i * unit : (i + 1) * unit] = (wide * wide).T.astype(BF16)

    return pl.pallas_call(
        body,
        grid=(steps,),
        out_shape=[jax.ShapeDtypeStruct((halves, part * unit, tokens), BF16) for part in parts],
        in_specs=in_specs + [ANY] * len(deps),
        out_specs=[
            pl.BlockSpec((halves, part // steps * unit, tokens), lambda j: (0, j, 0)) for part in parts
        ],
        compiler_params=pltpu.CompilerParams(vmem_limit_bytes=VMEM_LIMIT),
        cost_estimate=COST,
        name="cut",
    )(*ins, *deps)


def slot_call(plan, flags, last, fold=None, merge=None, gather=None, send=None, final=None, ahead=None, carry=None, cross=None, deps=()):
    unit = plan.unit
    ins, in_specs, outs, out_specs, aliases, kinds = [], [], [], [], {}, []
    most = lambda *some: max([part[0].units for part in some if part is not None] + [0])
    extra = lambda array: 0 if array is None else -(-array.shape[1] // unit)
    steps = max(
        most(final), most(merge, gather, send) + extra(carry), most(fold, merge) + extra(cross), 0 if ahead is None else AHEAD
    )

    def take(array, spec):
        ins.append(array)
        in_specs.append(spec)
        return len(ins) - 1

    def give(kind, shape, spec, dtype=BF16):
        outs.append(jax.ShapeDtypeStruct(shape, dtype))
        out_specs.append(spec)
        kinds.append(kind)
        return len(outs) - 1

    def at(piece, j):
        return jnp.minimum(j, piece.units - 1) if piece.units < steps else j

    def half_of(kind, flag):
        return {"sent": flag[0], "kept": 1 - flag[0]}.get(kind, kind)

    def rows_spec(piece, kind, width, column):
        return pl.BlockSpec(
            (unit, width),
            lambda j, flag: (half_of(kind, flag) * plan.units + piece.first + at(piece, j), column),
        )

    def half_spec(piece, kind):
        return pl.BlockSpec((None, unit, WIDTH), lambda j, flag: (half_of(kind, flag), at(piece, j), 0))

    def take_gsq(gsq, h):
        shape = (gsq.shape[0], None) + gsq.shape[2:]
        return take(gsq, pl.BlockSpec(shape, lambda j, flag: (0, h, 0, 0)))

    def give_long(kind, count, units, tail):
        total = units + extra(tail)
        last_block = total - 1
        out = give(
            kind,
            (count, units * unit + (0 if tail is None else tail.shape[1]), WIDTH),
            pl.BlockSpec((count, unit, WIDTH), lambda j, flag: (0, jnp.minimum(j, last_block), 0)),
        )
        if tail is None:
            return out, None
        blocks = extra(tail) - 1
        spec = pl.BlockSpec((2, unit, WIDTH), lambda j, flag: (0, jnp.clip(j - units, 0, blocks), 0))
        return out, (take(tail, spec), units, total)

    def take_side(piece, kind, tasks):
        ids = []
        squared, gsq = tasks
        for h, asq in enumerate(squared):
            if isinstance(asq, list):
                q, offset = plan.part_of(piece)
                array = asq[q]
                spec = pl.BlockSpec(
                    (array.shape[0], None, unit, array.shape[3]),
                    lambda j, flag: (0, half_of(kind, flag), offset + at(piece, j), 0),
                )
            else:
                array, spec = asq, rows_spec(piece, kind, asq.shape[1], 0)
            ids.append((take(array, spec), take_gsq(gsq, h)))
        return ids

    def take_other(piece, tasks):
        parts, gsq = tasks
        q, offset = plan.part_of(piece)
        array = parts[q]
        return [
            (
                take(
                    array,
                    pl.BlockSpec(
                        (array.shape[0], None, unit, array.shape[3]),
                        lambda j, flag, h=h: (0, h, offset + at(piece, j), 0),
                    ),
                ),
                take_gsq(gsq, h),
            )
            for h in range(gsq.shape[1])
        ]

    if fold is not None:
        piece, weight, received, side = fold
        fold_w = take(weight, rows_spec(piece, "sent", WIDTH, piece.group))
        fold_in = take(received, half_spec(piece, "sent"))
        fold_side = take_side(piece, "sent", side)
    if merge is not None:
        piece, weight, received, side, mean, other = merge
        merge_w = take(weight, rows_spec(piece, "kept", WIDTH, piece.group))
        merge_in = take(received, half_spec(piece, "kept"))
        merge_side = take_side(piece, "kept", side)
        merge_mean = take(mean, half_spec(piece, 0))
        merge_other = take_other(piece, other)
    apart = fold is not None and merge is not None and fold[0].units != merge[0].units
    if fold is not None or merge is not None:
        sections = 1 if fold is None or apart else 2
        across_out, across_tail = give_long("across", sections, most(merge if fold is None else fold), cross)
        back_out, back_place = across_out, sections - 1
        if apart:
            back_out, back_place = give_long("back", 1, most(merge), None)[0], 0
    outgoing = [part for part in (merge, gather) if part is not None]
    if outgoing or send is not None:
        if gather is not None:
            piece, came, section = gather
            gather_came = take(came, half_spec(piece, section))
        if send is not None:
            piece, inward, own = send
            if own:
                send_in = [take(inward, rows_spec(piece, h, WIDTH, piece.group)) for h in (0, 1)]
            else:
                send_in = [take(inward, half_spec(piece, h)) for h in (0, 1)]
        pass_count = 2 if send is not None or merge is not None else 1
        pass_out, pass_tail = give_long("pass", pass_count, most(merge, gather, send), carry)
    if final is not None:
        piece, kept, crossed, buffer, acts, total = final
        final_kept = [take(x, half_spec(piece, kept[2])) for x in kept[:2]]
        final_crossed = [take(x, half_spec(piece, crossed[2])) for x in crossed[:2]]
        first, group = piece.first, piece.group
        final_piece = piece
        final_out = give(
            "final",
            (2, plan.half, plan.cols),
            pl.BlockSpec((2, unit, WIDTH), lambda j, flag: (0, first + at(final_piece, j), group)),
        )
        if buffer is not None:
            aliases[1 + take(buffer, ANY)] = final_out
        if acts is not None:
            result_acts = [
                take(
                    acts,
                    pl.BlockSpec(
                        (acts.shape[0], unit),
                        lambda j, flag, h=h: (0, h * plan.units + first + at(final_piece, j)),
                    ),
                )
                for h in (0, 1)
            ]
            whole = pl.BlockSpec((acts.shape[0], WIDTH), lambda j, flag: (0, 0))
            result_in = None if total is None else take(total, whole)
            result_out = give("result", (acts.shape[0], WIDTH), whole, F32)
    if ahead is not None:
        ahead_acts, ahead_weight, ahead_group, ahead_turn, ahead_total = ahead
        tokens, depth = ahead_acts.shape[0], plan.rows // AHEAD**2
        block_at = lambda j: ahead_turn * AHEAD + jnp.minimum(j, AHEAD - 1)
        ahead_lhs = take(ahead_acts, pl.BlockSpec((tokens, depth), lambda j, flag: (0, block_at(j))))
        ahead_mat = take(ahead_weight, pl.BlockSpec((depth, WIDTH), lambda j, flag: (block_at(j), ahead_group)))
        everything = pl.BlockSpec((tokens, WIDTH), lambda j, flag: (0, 0))
        ahead_in = None if ahead_total is None else take(ahead_total, everything)
        ahead_out = give("ahead", (tokens, WIDTH), everything, F32)
    for dep in deps:
        take(dep, ANY)

    def body(flag, *refs):
        inr, outr = refs[: len(ins)], refs[len(ins) :]
        j = pl.program_id(0)

        def during(part, extra=True):
            units = part[0].units
            if units < steps:
                return pl.when((j < units) & extra)
            return pl.when(extra) if extra is not True else (lambda f: f())

        def fisher(task):
            ref = inr[task[0]]
            if len(ref.shape) == 3:
                asq = jnp.concatenate([ref[b] for b in range(ref.shape[0])], axis=1)
            else:
                asq = ref[...]
            gsq = inr[task[1]][...]
            return jnp.dot(asq, gsq.reshape(-1, gsq.shape[-1]), preferred_element_type=F32)

        def summed(tasks):
            return functools.reduce(lambda a, b: a + b, [fisher(task) for task in tasks])

        def follow(out, tail):
            ref, start, stop = tail

            @pl.when((j >= start) & (j < stop))
            def _():
                outr[out][...] = inr[ref][...]

        if carry is not None:
            follow(pass_out, pass_tail)
        if cross is not None:
            follow(across_out, across_tail)
        if send is not None:

            @during(send, flag[1] != last)
            def _():
                for h in (0, 1):
                    outr[pass_out][h] = inr[send_in[h]][...]

        if gather is not None:

            @during(gather, flag[1] == last)
            def _():
                outr[pass_out][pass_count - 1] = inr[gather_came][...]

        if final is not None:

            @during(final, flag[1] == last)
            def _():
                outr[final_out][1 - flag[0]] = inr[final_kept[0]][...]
                outr[final_out][flag[0]] = inr[final_crossed[0]][...]

            @during(final, flag[1] != last)
            def _():
                outr[final_out][1 - flag[0]] = inr[final_kept[1]][...]
                outr[final_out][flag[0]] = inr[final_crossed[1]][...]

        def add_to(out, before, value):
            @pl.when(j == 0)
            def _():
                outr[out][...] = value if before is None else inr[before][...] + value

            @pl.when(j > 0)
            def _():
                outr[out][...] += value

        if final is not None and final[4] is not None:

            @during(final)
            def _():
                parts = [
                    jnp.dot(inr[result_acts[h]][...], outr[final_out][h], preferred_element_type=F32)
                    for h in (0, 1)
                ]
                add_to(result_out, result_in, parts[0] + parts[1])

        if ahead is not None:

            @pl.when(j < AHEAD)
            def _():
                add_to(
                    ahead_out,
                    ahead_in,
                    jnp.dot(inr[ahead_lhs][...], inr[ahead_mat][...], preferred_element_type=F32),
                )

        if fold is not None:

            @during(fold)
            def _():
                here, before = fisher(fold_side[0]), summed(fold_side[1:])
                total = here + before
                mean = (here * inr[fold_w][...].astype(F32) + before * inr[fold_in][...].astype(F32)) / total
                outr[across_out][0] = jnp.where(total > 0, mean, 0.0).astype(BF16)

        if merge is not None:

            @during(merge)
            def _():
                here, before, there = fisher(merge_side[0]), summed(merge_side[1:]), summed(merge_other)
                numer = (
                    here * inr[merge_w][...].astype(F32)
                    + before * inr[merge_in][...].astype(F32)
                    + there * inr[merge_mean][...].astype(F32)
                )
                value = (numer / (here + before + there + 1e-6)).astype(BF16)
                outr[back_out][back_place] = value

                @pl.when(flag[1] == last)
                def _():
                    outr[pass_out][0] = value

    result = pl.pallas_call(
        body,
        grid_spec=pltpu.PrefetchScalarGridSpec(
            num_scalar_prefetch=1, grid=(steps,), in_specs=in_specs, out_specs=out_specs
        ),
        out_shape=outs,
        input_output_aliases=aliases,
        compiler_params=pltpu.CompilerParams(vmem_limit_bytes=VMEM_LIMIT),
        cost_estimate=COST,
        name="slot",
    )(flags, *ins)
    return dict(zip(kinds, result))


def local(sizes, activations, weights, labels, prototypes):
    tasks, rows_n, cols_n = sizes
    side_n = tasks // 2
    last = side_n - 1
    acts, weight, label_row, protos = activations[0], weights[0], labels[0], prototypes[0]
    block_tokens = acts.shape[0]
    tokens = block_tokens * cols_n
    share = tokens // rows_n
    plan = Plan(*weight.shape)
    place, row = lax.axis_index("task"), lax.axis_index("row")
    depth = jnp.minimum(place, tasks - 1 - place)
    sent = (place >= side_n).astype(jnp.int32)
    flags = jnp.stack([sent, depth.astype(jnp.int32)])

    mirrored = lambda pairs: pairs + [(tasks - 1 - a, tasks - 1 - b) for a, b in pairs]
    step_in = lambda d: mirrored([(d, d + 1)])
    step_out = lambda d: mirrored([(d + 1, d)])
    all_in = mirrored([(d, d + 1) for d in range(last)])
    send_in = lambda x: lax.ppermute(x, "task", all_in)
    send_mid = lambda x: lax.ppermute(x, "task", [(last, side_n), (side_n, last)])
    swap = lambda x: lax.ppermute(x, "task", step_in(last - 1) + step_out(last - 1))
    send_row = lambda x, s: lax.ppermute(x, "row", [(i, (i + s) % rows_n) for i in range(rows_n)])

    def sum_rows(full):
        cut_out = lambda r: lax.dynamic_slice_in_dim(full, r * share, share, 1)
        got = [send_row(cut_out((row + s) % rows_n), s) for s in range(1, rows_n)]
        total = cut_out(row).astype(F32)
        for part in got:
            total = total + part.astype(F32)
        return total

    def gather_rows(part):
        full = jnp.zeros((rows_n,) + part.shape, part.dtype)
        full = lax.dynamic_update_index_in_dim(full, part, row, 0)
        for s in range(1, rows_n):
            full = lax.dynamic_update_index_in_dim(full, send_row(part, s), (row - s) % rows_n, 0)
        return full

    full_acts = lax.all_gather(acts, "col", axis=0, tiled=True)

    crossing = lambda x: send_mid(lax.dynamic_slice_in_dim(x, sent * plan.half, plan.half, 1))
    near, cross = [acts], [crossing(acts)]
    for _ in range(last):
        near += tie([send_in(near[-1])], cross[-1:])
        cross.append(crossing(near[-1]))

    my_labels = lax.dynamic_slice_in_dim(label_row, row * share, share, 0)
    onehot = (my_labels[:, None] == lax.broadcasted_iota(jnp.int32, (share, protos.shape[0]), 1)).astype(BF16)
    target = jnp.dot(onehot, protos, preferred_element_type=F32)

    def squared_grad(product, group):
        groups = product.shape[0]
        wanted = target[:, group * WIDTH : (group + groups) * WIDTH].reshape(share, groups, WIDTH)
        grad = sum_rows(product) - jnp.moveaxis(wanted, 1, 0)
        return (grad * grad).astype(BF16)

    def packed(array):
        flat = array.reshape(-1, WIDTH)
        fill = -flat.shape[0] % 32
        return jnp.pad(flat, ((0, fill), (0, 0))).reshape(2, -1, WIDTH)

    def unpacked(array, shape):
        size = functools.reduce(lambda a, b: a * b, shape[:-1])
        rows = size + -size % 32
        return array[:, array.shape[1] - rows // 2 :].reshape(-1, WIDTH)[:size].reshape(shape)

    class Gradient:
        def __init__(self, group, groups):
            self.first, self.groups = group, groups
            self.outer, self.own, self.far, self.oth = ([None] * groups for _ in range(4))

        def start(self, product):
            self.near = [squared_grad(product, self.first)]
            for _ in range(last - 1):
                self.near.append(send_in(self.near[-1]))

        def inwards(self, g):
            return packed(jnp.stack([x[g] for x in self.near]))

        def inside(self, g, came):
            self.outer[g] = unpacked(came, (last, share, WIDTH))
            self.own[g] = gather_rows(jnp.concatenate([self.near[0][g][None], self.outer[g]]))

        def outside(self, g, part, came):
            came = unpacked(came, (last if part else 1, share, WIDTH))
            if part:
                self.oth[g] = gather_rows(jnp.concatenate([self.far[g], came]))
            else:
                self.far[g] = came

    count = len(plan.pieces)
    batches = [Gradient(0, 1)]
    while batches[-1].first + batches[-1].groups < plan.groups:
        group = batches[-1].first + batches[-1].groups
        batches.append(Gradient(group, 1))
    batch_of = {b.first + g: b for b in batches for g in range(b.groups)}
    own_of = lambda piece: batch_of[piece.group].own[piece.group - batch_of[piece.group].first]
    other_of = lambda piece: batch_of[piece.group].oth[piece.group - batch_of[piece.group].first]

    def inward(index):
        piece = plan.pieces[index]
        if last == 1:
            return (piece, weight, True)
        a, b = piece.first * plan.unit, (piece.first + piece.units) * plan.unit
        q, offset = plan.part_of(piece)
        offset *= plan.unit
        columns = slice(piece.group * WIDTH, (piece.group + 1) * WIDTH)
        mine = weight.reshape(2, plan.half, plan.cols)[:, a:b, columns]
        squared = [own_square.reshape(2, plan.half, tokens)[:, a:b]]
        for task in outer_parts[: last - 1]:
            blocks = task[q][:, :, offset : offset + b - a]
            squared.append(jnp.moveaxis(blocks, 0, 2).reshape(2, b - a, tokens))
        gsq = jnp.moveaxis(own_of(piece), 0, 1).reshape(side_n, tokens, WIDTH)
        shares = [
            jnp.einsum("hrt,tc->hrc", s, g, preferred_element_type=F32)
            for s, g in zip(squared, gsq)
        ]
        mean, before = mine, jnp.zeros(mine.shape, F32)
        for d in range(1, last):
            came = lax.ppermute(mean, "task", step_in(d - 1)).astype(F32)
            before = before + shares[d]
            total = shares[0] + before
            value = (shares[0] * mine.astype(F32) + before * came) / total
            mean = jnp.where(depth == 0, mine, jnp.where(total > 0, value, 0.0).astype(BF16))
        return (piece, mean, False)

    def outward(came):
        for d in reversed(range(last - 1)):
            arrived = lax.ppermute(came, "task", step_out(d))
            came = jnp.where(depth == d, arrived, came)
        return came

    sent_pass, came_pass, came_out = {}, {}, {}

    def start_pass(slot, got):
        if "pass" in got:
            sent_pass[slot] = got["pass"]
            came_pass[slot] = swap(got["pass"])
            came_out[slot] = outward(came_pass[slot])

    if last == 1:
        start_pass(-2, slot_call(plan, flags, last, send=inward(0), deps=[near[-1], cross[0]]))
    lead = batches[0]
    outer_cuts = [cut(plan, [task], list(sent_pass.values())) for task in near[1:]]
    product = group_product(full_acts, weight, 0, 1, deps=[x[0] for x in outer_cuts])
    gather_col = lambda x: lax.all_gather(x, "col", axis=0)
    outer_parts = [[gather_col(x) for x in task] for task in outer_cuts]

    def at_once(b, product):
        b.start(product)
        came = swap(jnp.stack(b.near))
        b.outer = [came[:, g] for g in range(b.groups)]
        stacked = jnp.concatenate([b.near[0][None], came])
        crossed = send_mid(stacked)
        b.own = [gather_rows(stacked[:, g]) for g in range(b.groups)]
        b.oth = [gather_rows(crossed[:, g]) for g in range(b.groups)]
        return crossed

    lead_far = at_once(lead, product)
    own_square = squares(full_acts, [lead.near[0]])
    carries, crossings, starts = {}, {}, {}

    def ship(slot, b):
        for g in range(b.groups):
            carries[slot + g] = (b, g)
            crossings[slot + g] = (b, g, 0)
            crossings[slot + LAG + g] = (b, g, 1)

    if last == 1 and count > 1:
        start_pass(-1, slot_call(plan, flags, last, send=inward(1), deps=[own_square, lead.outer[0]] + list(came_pass.values())))
    other_cuts = cut(plan, cross, [own_square] + list(sent_pass.values())[-1:])
    other_parts = [gather_col(x) for x in other_cuts]
    early = min(LAG, plan.groups - 1) if last == 1 else plan.groups - 1
    deps = [other_cuts[0], lead.outer[0]] + list(sent_pass.values())[-1:]
    next_products = group_product(full_acts, weight, 1, early, deps=deps)
    fused = last == 1 and plan.unit % 128 == 0 and plan.rows % (AHEAD**2 * 128) == 0
    first_of = lambda b: min(i for i, p in enumerate(plan.pieces) if p.group == b.first)
    rest = list(batches[1:])
    if fused and all(first_of(b) >= AHEAD * (i + 1) for i, b in enumerate(rest)):
        for slot, b in enumerate(rest[:LAG]):
            b.start(next_products[slot : slot + 1])
            ship(slot, b)
        turn = 0
        for b in rest[LAG:]:
            starts.update({turn + k: (b, k) for k in range(AHEAD)})
            turn += AHEAD
            slot = turn
            while {slot, slot + LAG} & set(crossings):
                slot += 1
            ship(slot, b)
    else:
        for i, b in enumerate(rest):
            at_once(b, next_products[i : i + 1])
    if last > 1:
        for index in range(min(LAG, count)):
            start_pass(index - LAG, slot_call(plan, flags, last, send=inward(index)))

    came_mid, backs = {}, {}
    buffer = None
    results = []
    chain = [next_products, lead_far]
    ahead_total, result_total = None, None
    for slot in range(count + 3 * LAG):
        deps = list(chain)
        stage = {}
        now = lambda index: 0 <= index < count
        side_of = lambda piece: ([own_square] + outer_parts, own_of(piece))
        if slot - LAG in carries:
            b, g = carries[slot - LAG]
            b.inside(g, came_pass[slot - LAG])
        if slot - LAG in crossings:
            b, g, part = crossings[slot - LAG]
            b.outside(g, part, came_mid[slot - LAG])
        if slot in crossings:
            b, g, part = crossings[slot]
            stage["cross"] = packed(b.outer[g] if part else b.near[0][g])
        if slot in carries:
            b, g = carries[slot]
            stage["carry"] = b.inwards(g)
        if now(slot):
            piece = plan.pieces[slot]
            stage["fold"] = (piece, weight, came_pass[slot - LAG], side_of(piece))
        if now(slot + LAG):
            stage["send"] = inward(slot + LAG)
        if slot < max(carries, default=0):
            stage.setdefault("cross", packed(lead.near[0][0]))
            if slot == 0:
                stage.setdefault("carry", lead.inwards(0))
        index = slot - LAG
        if now(index):
            piece = plan.pieces[index]
            stage["merge"] = (
                piece,
                weight,
                came_pass[index - LAG],
                side_of(piece),
                came_mid[index],
                (other_parts, other_of(piece)),
            )
        index = slot - 2 * LAG
        if now(index):
            stage["gather"] = (plan.pieces[index],) + backs[slot - LAG]
        index = slot - 3 * LAG
        if now(index):
            stage["final"] = (
                plan.pieces[index],
                (sent_pass[slot - 2 * LAG], came_out[slot - 2 * LAG], 0),
                (sent_pass[slot - LAG], came_out[slot - LAG], sent_pass[slot - LAG].shape[0] - 1),
                buffer,
                full_acts if fused else None,
                result_total,
            )
        if slot in starts:
            b, turn = starts[slot]
            stage["ahead"] = (full_acts, weight, b.first, turn, ahead_total)
        got = slot_call(plan, flags, last, deps=deps, **stage)
        chain = [got[name] for name in ("across", "pass") if name in got][:1]
        if "across" in got:
            came_mid[slot] = send_mid(got["across"])
            backs[slot] = (came_mid[slot], got["across"].shape[0] - 1)
            if "back" in got:
                backs[slot] = (send_mid(got["back"]), 0)
        start_pass(slot, got)
        if "final" in got:
            buffer = got["final"]
            done = plan.pieces[slot - 3 * LAG]
            result_total = got.get("result")
            if done.first + done.units == plan.units:
                if fused:
                    out = result_total.astype(BF16)[None]
                else:
                    out = group_product(full_acts, buffer.reshape(plan.rows, plan.cols), done.group, 1)
                results.append(sum_rows(out).astype(BF16))
                result_total = None
        if "ahead" in got:
            ahead_total = got["ahead"]
            b, turn = starts[slot]
            if turn == AHEAD - 1:
                b.start(ahead_total.astype(BF16)[None])
                ahead_total = None
    result = jnp.moveaxis(jnp.concatenate(results), 0, 1).reshape(1, share, plan.cols)
    return buffer.reshape(plan.rows, plan.cols), result


def solution(mesh):
    placed = (
        P("task", "col", "row"),
        P("task", "row", "col"),
        P("task", None),
        P("task", None, "col"),
    )
    sizes = (mesh.shape["task"], mesh.shape["row"], mesh.shape["col"])
    return jax.shard_map(
        functools.partial(local, sizes),
        mesh=mesh,
        in_specs=placed,
        out_specs=(P("row", "col"), P("task", "row", "col")),
        check_vma=False,
    )
```

```python
import functools

import jax
import jax.numpy as jnp
from jax import lax
from jax.experimental import pallas as pl
from jax.experimental.pallas import tpu as pltpu
from jax.sharding import PartitionSpec as P

BF16 = jnp.bfloat16
F32 = jnp.float32
ANY = pl.BlockSpec(memory_space=pl.ANY)
WIDTH = 256
UNIT_ROWS = 384
MOST = 3
AHEAD = 3
LAG = 2
VMEM_LIMIT = 60 * 1024 * 1024
COST = pl.CostEstimate(flops=0, bytes_accessed=0, transcendentals=0)


def largest_divisor(total, limit, unit):
    best = total
    for size in range(unit, limit + 1, unit):
        if total % size == 0:
            best = size
    return best


def tie(arrays, deps):
    count = len(arrays)

    def body(*refs):
        pass

    return pl.pallas_call(
        body,
        out_shape=[jax.ShapeDtypeStruct(x.shape, x.dtype) for x in arrays],
        in_specs=[ANY] * (count + len(deps)),
        out_specs=[ANY] * count,
        input_output_aliases={i: i for i in range(count)},
        cost_estimate=COST,
        name="tie",
    )(*arrays, *deps)


def group_product(lhs, mat, group, groups, deps=()):
    tokens, rows = lhs.shape
    depth = largest_divisor(rows, 1152, 128)
    steps = rows // depth

    def body(lhs_ref, *rest):
        mats, (out_ref, acc_ref) = rest[:groups], rest[-2:]
        step = pl.program_id(0)
        wide = jnp.concatenate([mat[...] for mat in mats], axis=1) if groups > 1 else mats[0][...]
        part = jnp.dot(lhs_ref[...], wide, preferred_element_type=F32)

        @pl.when(step == 0)
        def _():
            acc_ref[...] = part

        @pl.when(step > 0)
        def _():
            acc_ref[...] += part

        @pl.when(step == steps - 1)
        def _():
            for g in range(groups):
                out_ref[g] = acc_ref[:, g * WIDTH : (g + 1) * WIDTH].astype(BF16)

    return pl.pallas_call(
        body,
        grid=(steps,),
        out_shape=jax.ShapeDtypeStruct((groups, tokens, WIDTH), BF16),
        in_specs=[pl.BlockSpec((tokens, depth), lambda k: (0, k))]
        + [pl.BlockSpec((depth, WIDTH), lambda k, g=g: (k, group + g)) for g in range(groups)]
        + [ANY] * len(deps),
        out_specs=pl.BlockSpec((groups, tokens, WIDTH), lambda k: (0, 0, 0)),
        scratch_shapes=[pltpu.VMEM((tokens, groups * WIDTH), F32)],
        compiler_params=pltpu.CompilerParams(vmem_limit_bytes=VMEM_LIMIT),
        cost_estimate=COST,
        name="group_product",
    )(lhs, *[mat] * groups, *deps)


def squares(acts, deps):
    tokens, rows = acts.shape
    depth = largest_divisor(rows, 768, 128)

    def body(acts_ref, *rest):
        wide = acts_ref[...].astype(F32)
        rest[-1][...] = (wide * wide).astype(BF16).T

    return pl.pallas_call(
        body,
        grid=(rows // depth,),
        out_shape=jax.ShapeDtypeStruct((rows, tokens), BF16),
        in_specs=[pl.BlockSpec((tokens, depth), lambda k: (0, k))] + [ANY] * len(deps),
        out_specs=pl.BlockSpec((depth, tokens), lambda k: (k, 0)),
        compiler_params=pltpu.CompilerParams(vmem_limit_bytes=VMEM_LIMIT),
        cost_estimate=COST,
        name="squares",
    )(acts, *deps)


class Piece:
    def __init__(self, group, first, units, place):
        self.group, self.first, self.units, self.place = group, first, units, place


class Plan:
    def __init__(self, rows, cols):
        self.rows, self.cols = rows, cols
        self.half = rows // 2
        self.groups = cols // WIDTH
        self.unit = largest_divisor(self.half, UNIT_ROWS, 16)
        self.units = self.half // self.unit
        lead = largest_divisor(self.units, MOST, 1)
        self.bounds = [(0, self.units)]
        self.pieces = []
        for group in range(self.groups):
            first = 0
            while first < self.units:
                left = self.units - first
                units = min(lead, left)
                self.pieces.append(Piece(group, first, units, len([p for p in self.pieces if p.group == group])))
                first += units

    def part_of(self, piece):
        q = [a <= piece.first < b for a, b in self.bounds].index(True)
        return q, piece.first - self.bounds[q][0]


def cut(plan, tasks, deps):
    unit, tokens = plan.unit, tasks[0].shape[0]
    parts = [b - a for a, b in plan.bounds]
    halves = sum(task.shape[1] // plan.half for task in tasks)
    steps = MOST
    if unit % 128 or any(part % steps for part in parts):
        wide = jnp.concatenate(tasks, axis=1).astype(F32)
        whole = (wide * wide).astype(BF16).T.reshape(halves, plan.half, tokens)
        return [whole[:, a * unit : b * unit] for a, b in plan.bounds]
    ins, in_specs, places = [], [], []
    count = 0
    for task in tasks:
        for h in range(task.shape[1] // plan.half):
            for q, (a, b) in enumerate(plan.bounds):
                per = (b - a) // steps
                for i in range(per):
                    first = h * plan.units + a + i
                    ins.append(task)
                    in_specs.append(
                        pl.BlockSpec((tokens, unit), lambda j, first=first, per=per: (0, first + per * j))
                    )
                    places.append((q, count, i))
            count += 1

    def body(*refs):
        outs = refs[len(refs) - len(parts) :]
        for ref, (q, h, i) in zip(refs, places):
            wide = ref[...].astype(F32)
            outs[q][h, i * unit : (i + 1) * unit] = (wide * wide).T.astype(BF16)

    return pl.pallas_call(
        body,
        grid=(steps,),
        out_shape=[jax.ShapeDtypeStruct((halves, part * unit, tokens), BF16) for part in parts],
        in_specs=in_specs + [ANY] * len(deps),
        out_specs=[
            pl.BlockSpec((halves, part // steps * unit, tokens), lambda j: (0, j, 0)) for part in parts
        ],
        compiler_params=pltpu.CompilerParams(vmem_limit_bytes=VMEM_LIMIT),
        cost_estimate=COST,
        name="cut",
    )(*ins, *deps)


def slot_call(plan, flags, last, fold=None, merge=None, gather=None, send=None, final=None, ahead=None, carry=None, cross=None, deps=()):
    unit = plan.unit
    ins, in_specs, outs, out_specs, aliases, kinds = [], [], [], [], {}, []
    most = lambda *some: max([part[0].units for part in some if part is not None] + [0])
    extra = lambda array: 0 if array is None else -(-array.shape[1] // unit)
    steps = max(
        most(final), most(merge, gather, send) + extra(carry), most(fold, merge) + extra(cross), 0 if ahead is None else AHEAD
    )

    def take(array, spec):
        ins.append(array)
        in_specs.append(spec)
        return len(ins) - 1

    def give(kind, shape, spec, dtype=BF16):
        outs.append(jax.ShapeDtypeStruct(shape, dtype))
        out_specs.append(spec)
        kinds.append(kind)
        return len(outs) - 1

    def at(piece, j):
        return jnp.minimum(j, piece.units - 1) if piece.units < steps else j

    def half_of(kind, flag):
        return {"sent": flag[0], "kept": 1 - flag[0]}.get(kind, kind)

    def rows_spec(piece, kind, width, column):
        return pl.BlockSpec(
            (unit, width),
            lambda j, flag: (half_of(kind, flag) * plan.units + piece.first + at(piece, j), column),
        )

    def half_spec(piece, kind):
        return pl.BlockSpec((None, unit, WIDTH), lambda j, flag: (half_of(kind, flag), at(piece, j), 0))

    def take_gsq(gsq, h):
        shape = (gsq.shape[0], None) + gsq.shape[2:]
        return take(gsq, pl.BlockSpec(shape, lambda j, flag: (0, h, 0, 0)))

    def give_long(kind, count, units, tail):
        total = units + extra(tail)
        last_block = total - 1
        out = give(
            kind,
            (count, units * unit + (0 if tail is None else tail.shape[1]), WIDTH),
            pl.BlockSpec((count, unit, WIDTH), lambda j, flag: (0, jnp.minimum(j, last_block), 0)),
        )
        if tail is None:
            return out, None
        blocks = extra(tail) - 1
        spec = pl.BlockSpec((2, unit, WIDTH), lambda j, flag: (0, jnp.clip(j - units, 0, blocks), 0))
        return out, (take(tail, spec), units, total)

    def take_side(piece, kind, tasks):
        ids = []
        squared, gsq = tasks
        for h, asq in enumerate(squared):
            if isinstance(asq, list):
                q, offset = plan.part_of(piece)
                array = asq[q]
                spec = pl.BlockSpec(
                    (array.shape[0], None, unit, array.shape[3]),
                    lambda j, flag: (0, half_of(kind, flag), offset + at(piece, j), 0),
                )
            else:
                array, spec = asq, rows_spec(piece, kind, asq.shape[1], 0)
            ids.append((take(array, spec), take_gsq(gsq, h)))
        return ids

    def take_other(piece, tasks):
        parts, gsq = tasks
        q, offset = plan.part_of(piece)
        array = parts[q]
        return [
            (
                take(
                    array,
                    pl.BlockSpec(
                        (array.shape[0], None, unit, array.shape[3]),
                        lambda j, flag, h=h: (0, h, offset + at(piece, j), 0),
                    ),
                ),
                take_gsq(gsq, h),
            )
            for h in range(gsq.shape[1])
        ]

    if fold is not None:
        piece, weight, received, side = fold
        fold_w = take(weight, rows_spec(piece, "sent", WIDTH, piece.group))
        fold_in = take(received, half_spec(piece, "sent"))
        fold_side = take_side(piece, "sent", side)
    if merge is not None:
        piece, weight, received, side, mean, other = merge
        merge_w = take(weight, rows_spec(piece, "kept", WIDTH, piece.group))
        merge_in = take(received, half_spec(piece, "kept"))
        merge_side = take_side(piece, "kept", side)
        merge_mean = take(mean, half_spec(piece, 0))
        merge_other = take_other(piece, other)
    apart = fold is not None and merge is not None and fold[0].units != merge[0].units
    if fold is not None or merge is not None:
        sections = 1 if fold is None or apart else 2
        across_out, across_tail = give_long("across", sections, most(merge if fold is None else fold), cross)
        back_out, back_place = across_out, sections - 1
        if apart:
            back_out, back_place = give_long("back", 1, most(merge), None)[0], 0
    outgoing = [part for part in (merge, gather) if part is not None]
    if outgoing or send is not None:
        if gather is not None:
            piece, came, section = gather
            gather_came = take(came, half_spec(piece, section))
        if send is not None:
            piece, inward, own = send
            if own:
                send_in = [take(inward, rows_spec(piece, h, WIDTH, piece.group)) for h in (0, 1)]
            else:
                send_in = [take(inward, half_spec(piece, h)) for h in (0, 1)]
        pass_count = 2 if send is not None or merge is not None else 1
        pass_out, pass_tail = give_long("pass", pass_count, most(merge, gather, send), carry)
    if final is not None:
        piece, kept, crossed, buffer, acts, total = final
        final_kept = [take(x, half_spec(piece, kept[2])) for x in kept[:2]]
        final_crossed = [take(x, half_spec(piece, crossed[2])) for x in crossed[:2]]
        first, group = piece.first, piece.group
        final_piece = piece
        final_out = give(
            "final",
            (2, plan.half, plan.cols),
            pl.BlockSpec((2, unit, WIDTH), lambda j, flag: (0, first + at(final_piece, j), group)),
        )
        if buffer is not None:
            aliases[1 + take(buffer, ANY)] = final_out
        if acts is not None:
            result_acts = [
                take(
                    acts,
                    pl.BlockSpec(
                        (acts.shape[0], unit),
                        lambda j, flag, h=h: (0, h * plan.units + first + at(final_piece, j)),
                    ),
                )
                for h in (0, 1)
            ]
            whole = pl.BlockSpec((acts.shape[0], WIDTH), lambda j, flag: (0, 0))
            result_in = None if total is None else take(total, whole)
            result_out = give("result", (acts.shape[0], WIDTH), whole, F32)
    if ahead is not None:
        ahead_acts, ahead_weight, ahead_group, ahead_turn, ahead_total = ahead
        tokens, depth = ahead_acts.shape[0], plan.rows // AHEAD**2
        block_at = lambda j: ahead_turn * AHEAD + jnp.minimum(j, AHEAD - 1)
        ahead_lhs = take(ahead_acts, pl.BlockSpec((tokens, depth), lambda j, flag: (0, block_at(j))))
        ahead_mat = take(ahead_weight, pl.BlockSpec((depth, WIDTH), lambda j, flag: (block_at(j), ahead_group)))
        everything = pl.BlockSpec((tokens, WIDTH), lambda j, flag: (0, 0))
        ahead_in = None if ahead_total is None else take(ahead_total, everything)
        ahead_out = give("ahead", (tokens, WIDTH), everything, F32)
    for dep in deps:
        take(dep, ANY)

    def body(flag, *refs):
        inr, outr = refs[: len(ins)], refs[len(ins) :]
        j = pl.program_id(0)

        def during(part, extra=True):
            units = part[0].units
            if units < steps:
                return pl.when((j < units) & extra)
            return pl.when(extra) if extra is not True else (lambda f: f())

        def fisher(task):
            ref = inr[task[0]]
            if len(ref.shape) == 3:
                asq = jnp.concatenate([ref[b] for b in range(ref.shape[0])], axis=1)
            else:
                asq = ref[...]
            gsq = inr[task[1]][...]
            return jnp.dot(asq, gsq.reshape(-1, gsq.shape[-1]), preferred_element_type=F32)

        def summed(tasks):
            return functools.reduce(lambda a, b: a + b, [fisher(task) for task in tasks])

        def follow(out, tail):
            ref, start, stop = tail

            @pl.when((j >= start) & (j < stop))
            def _():
                outr[out][...] = inr[ref][...]

        if carry is not None:
            follow(pass_out, pass_tail)
        if cross is not None:
            follow(across_out, across_tail)
        if send is not None:

            @during(send, flag[1] != last)
            def _():
                for h in (0, 1):
                    outr[pass_out][h] = inr[send_in[h]][...]

        if gather is not None:

            @during(gather, flag[1] == last)
            def _():
                outr[pass_out][pass_count - 1] = inr[gather_came][...]

        if final is not None:

            @during(final, flag[1] == last)
            def _():
                outr[final_out][1 - flag[0]] = inr[final_kept[0]][...]
                outr[final_out][flag[0]] = inr[final_crossed[0]][...]

            @during(final, flag[1] != last)
            def _():
                outr[final_out][1 - flag[0]] = inr[final_kept[1]][...]
                outr[final_out][flag[0]] = inr[final_crossed[1]][...]

        def add_to(out, before, value):
            @pl.when(j == 0)
            def _():
                outr[out][...] = value if before is None else inr[before][...] + value

            @pl.when(j > 0)
            def _():
                outr[out][...] += value

        if final is not None and final[4] is not None:

            @during(final)
            def _():
                parts = [
                    jnp.dot(inr[result_acts[h]][...], outr[final_out][h], preferred_element_type=F32)
                    for h in (0, 1)
                ]
                add_to(result_out, result_in, parts[0] + parts[1])

        if ahead is not None:

            @pl.when(j < AHEAD)
            def _():
                add_to(
                    ahead_out,
                    ahead_in,
                    jnp.dot(inr[ahead_lhs][...], inr[ahead_mat][...], preferred_element_type=F32),
                )

        if fold is not None:

            @during(fold)
            def _():
                here, before = fisher(fold_side[0]), summed(fold_side[1:])
                total = here + before
                mean = (here * inr[fold_w][...].astype(F32) + before * inr[fold_in][...].astype(F32)) / total
                outr[across_out][0] = jnp.where(total > 0, mean, 0.0).astype(BF16)

        if merge is not None:

            @during(merge)
            def _():
                here, before, there = fisher(merge_side[0]), summed(merge_side[1:]), summed(merge_other)
                numer = (
                    here * inr[merge_w][...].astype(F32)
                    + before * inr[merge_in][...].astype(F32)
                    + there * inr[merge_mean][...].astype(F32)
                )
                value = (numer / (here + before + there + 1e-6)).astype(BF16)
                outr[back_out][back_place] = value

                @pl.when(flag[1] == last)
                def _():
                    outr[pass_out][0] = value

    result = pl.pallas_call(
        body,
        grid_spec=pltpu.PrefetchScalarGridSpec(
            num_scalar_prefetch=1, grid=(steps,), in_specs=in_specs, out_specs=out_specs
        ),
        out_shape=outs,
        input_output_aliases=aliases,
        compiler_params=pltpu.CompilerParams(vmem_limit_bytes=VMEM_LIMIT),
        cost_estimate=COST,
        name="slot",
    )(flags, *ins)
    return dict(zip(kinds, result))


def local(sizes, activations, weights, labels, prototypes):
    tasks, rows_n, cols_n = sizes
    side_n = tasks // 2
    last = side_n - 1
    acts, weight, label_row, protos = activations[0], weights[0], labels[0], prototypes[0]
    block_tokens = acts.shape[0]
    tokens = block_tokens * cols_n
    share = tokens // rows_n
    plan = Plan(*weight.shape)
    place, row = lax.axis_index("task"), lax.axis_index("row")
    depth = jnp.minimum(place, tasks - 1 - place)
    sent = (place >= side_n).astype(jnp.int32)
    flags = jnp.stack([sent, depth.astype(jnp.int32)])

    mirrored = lambda pairs: pairs + [(tasks - 1 - a, tasks - 1 - b) for a, b in pairs]
    step_in = lambda d: mirrored([(d, d + 1)])
    step_out = lambda d: mirrored([(d + 1, d)])
    all_in = mirrored([(d, d + 1) for d in range(last)])
    send_in = lambda x: lax.ppermute(x, "task", all_in)
    send_mid = lambda x: lax.ppermute(x, "task", [(last, side_n), (side_n, last)])
    swap = lambda x: lax.ppermute(x, "task", step_in(last - 1) + step_out(last - 1))
    send_row = lambda x, s: lax.ppermute(x, "row", [(i, (i + s) % rows_n) for i in range(rows_n)])

    def sum_rows(full):
        cut_out = lambda r: lax.dynamic_slice_in_dim(full, r * share, share, 1)
        got = [send_row(cut_out((row + s) % rows_n), s) for s in range(1, rows_n)]
        total = cut_out(row).astype(F32)
        for part in got:
            total = total + part.astype(F32)
        return total

    def gather_rows(part):
        full = jnp.zeros((rows_n,) + part.shape, part.dtype)
        full = lax.dynamic_update_index_in_dim(full, part, row, 0)
        for s in range(1, rows_n):
            full = lax.dynamic_update_index_in_dim(full, send_row(part, s), (row - s) % rows_n, 0)
        return full

    full_acts = lax.all_gather(acts, "col", axis=0, tiled=True)

    crossing = lambda x: send_mid(lax.dynamic_slice_in_dim(x, sent * plan.half, plan.half, 1))
    near, cross = [acts], [crossing(acts)]
    for _ in range(last):
        near += tie([send_in(near[-1])], cross[-1:])
        cross.append(crossing(near[-1]))

    my_labels = lax.dynamic_slice_in_dim(label_row, row * share, share, 0)
    onehot = (my_labels[:, None] == lax.broadcasted_iota(jnp.int32, (share, protos.shape[0]), 1)).astype(BF16)
    target = jnp.dot(onehot, protos, preferred_element_type=F32)

    def squared_grad(product, group):
        groups = product.shape[0]
        wanted = target[:, group * WIDTH : (group + groups) * WIDTH].reshape(share, groups, WIDTH)
        grad = sum_rows(product) - jnp.moveaxis(wanted, 1, 0)
        return (grad * grad).astype(BF16)

    def packed(array):
        flat = array.reshape(-1, WIDTH)
        fill = -flat.shape[0] % 32
        return jnp.pad(flat, ((0, fill), (0, 0))).reshape(2, -1, WIDTH)

    def unpacked(array, shape):
        size = functools.reduce(lambda a, b: a * b, shape[:-1])
        rows = size + -size % 32
        return array[:, array.shape[1] - rows // 2 :].reshape(-1, WIDTH)[:size].reshape(shape)

    class Gradient:
        def __init__(self, group, groups):
            self.first, self.groups = group, groups
            self.outer, self.own, self.far, self.oth = ([None] * groups for _ in range(4))

        def start(self, product):
            self.near = [squared_grad(product, self.first)]
            for _ in range(last - 1):
                self.near.append(send_in(self.near[-1]))

        def inwards(self, g):
            return packed(jnp.stack([x[g] for x in self.near]))

        def inside(self, g, came):
            self.outer[g] = unpacked(came, (last, share, WIDTH))
            self.own[g] = gather_rows(jnp.concatenate([self.near[0][g][None], self.outer[g]]))

        def outside(self, g, part, came):
            came = unpacked(came, (last if part else 1, share, WIDTH))
            if part:
                self.oth[g] = gather_rows(jnp.concatenate([self.far[g], came]))
            else:
                self.far[g] = came

    count = len(plan.pieces)
    batches = [Gradient(0, 1)]
    while batches[-1].first + batches[-1].groups < plan.groups:
        group = batches[-1].first + batches[-1].groups
        batches.append(Gradient(group, 1))
    batch_of = {b.first + g: b for b in batches for g in range(b.groups)}
    own_of = lambda piece: batch_of[piece.group].own[piece.group - batch_of[piece.group].first]
    other_of = lambda piece: batch_of[piece.group].oth[piece.group - batch_of[piece.group].first]

    def inward(index):
        piece = plan.pieces[index]
        if last == 1:
            return (piece, weight, True)
        a, b = piece.first * plan.unit, (piece.first + piece.units) * plan.unit
        q, offset = plan.part_of(piece)
        offset *= plan.unit
        columns = slice(piece.group * WIDTH, (piece.group + 1) * WIDTH)
        mine = weight.reshape(2, plan.half, plan.cols)[:, a:b, columns]
        squared = [own_square.reshape(2, plan.half, tokens)[:, a:b]]
        for task in outer_parts[: last - 1]:
            blocks = task[q][:, :, offset : offset + b - a]
            squared.append(jnp.moveaxis(blocks, 0, 2).reshape(2, b - a, tokens))
        gsq = jnp.moveaxis(own_of(piece), 0, 1).reshape(side_n, tokens, WIDTH)
        shares = [
            jnp.einsum("hrt,tc->hrc", s, g, preferred_element_type=F32)
            for s, g in zip(squared, gsq)
        ]
        mean, before = mine, jnp.zeros(mine.shape, F32)
        for d in range(1, last):
            came = lax.ppermute(mean, "task", step_in(d - 1)).astype(F32)
            before = before + shares[d]
            total = shares[0] + before
            value = (shares[0] * mine.astype(F32) + before * came) / total
            mean = jnp.where(depth == 0, mine, jnp.where(total > 0, value, 0.0).astype(BF16))
        return (piece, mean, False)

    def outward(came):
        for d in reversed(range(last - 1)):
            arrived = lax.ppermute(came, "task", step_out(d))
            came = jnp.where(depth == d, arrived, came)
        return came

    sent_pass, came_pass, came_out = {}, {}, {}

    def start_pass(slot, got):
        if "pass" in got:
            sent_pass[slot] = got["pass"]
            came_pass[slot] = swap(got["pass"])
            came_out[slot] = outward(came_pass[slot])

    if last == 1:
        start_pass(-2, slot_call(plan, flags, last, send=inward(0), deps=[near[-1], cross[0]]))
    lead = batches[0]
    outer_cuts = [cut(plan, [task], list(sent_pass.values())) for task in near[1:]]
    rest = list(batches[1:])
    first_of = lambda b: min(i for i, p in enumerate(plan.pieces) if p.group == b.first)
    fused = last == 1 and plan.unit % 128 == 0 and plan.rows % (AHEAD**2 * 128) == 0
    fused = fused and all(first_of(b) >= AHEAD * (i + 1) for i, b in enumerate(rest))
    early = 1 + (min(LAG, len(rest)) if fused else len(rest))
    products = group_product(full_acts, weight, 0, early, deps=[x[0] for x in outer_cuts])
    gather_col = lambda x: lax.all_gather(x, "col", axis=0)
    outer_parts = [[gather_col(x) for x in task] for task in outer_cuts]

    def at_once(b, product):
        b.start(product)
        came = swap(jnp.stack(b.near))
        b.outer = [came[:, g] for g in range(b.groups)]
        stacked = jnp.concatenate([b.near[0][None], came])
        crossed = send_mid(stacked)
        b.own = [gather_rows(stacked[:, g]) for g in range(b.groups)]
        b.oth = [gather_rows(crossed[:, g]) for g in range(b.groups)]
        return crossed

    lead_far = at_once(lead, products[:1])
    own_square = squares(full_acts, [lead.near[0]])
    carries, crossings, starts = {}, {}, {}

    def ship(slot, b):
        for g in range(b.groups):
            carries[slot + g] = (b, g)
            crossings[slot + g] = (b, g, 0)
            crossings[slot + LAG + g] = (b, g, 1)

    if last == 1 and count > 1:
        start_pass(-1, slot_call(plan, flags, last, send=inward(1), deps=[own_square, lead.outer[0]] + list(came_pass.values())))
    other_cuts = cut(plan, cross, [own_square] + list(sent_pass.values())[-1:])
    other_parts = [gather_col(x) for x in other_cuts]
    if fused:
        for slot, b in enumerate(rest[:LAG]):
            b.start(products[1 + slot : 2 + slot])
            ship(slot, b)
        turn = 0
        for b in rest[LAG:]:
            starts.update({turn + k: (b, k) for k in range(AHEAD)})
            turn += AHEAD
            slot = turn
            while {slot, slot + LAG} & set(crossings):
                slot += 1
            ship(slot, b)
    else:
        for i, b in enumerate(rest):
            at_once(b, products[1 + i : 2 + i])
    if last > 1:
        for index in range(min(LAG, count)):
            start_pass(index - LAG, slot_call(plan, flags, last, send=inward(index)))

    came_mid, backs = {}, {}
    buffer = None
    results = []
    chain = [other_cuts[0], lead_far]
    ahead_total, result_total = None, None
    for slot in range(count + 3 * LAG):
        deps = list(chain)
        stage = {}
        now = lambda index: 0 <= index < count
        side_of = lambda piece: ([own_square] + outer_parts, own_of(piece))
        if slot - LAG in carries:
            b, g = carries[slot - LAG]
            b.inside(g, came_pass[slot - LAG])
        if slot - LAG in crossings:
            b, g, part = crossings[slot - LAG]
            b.outside(g, part, came_mid[slot - LAG])
        if slot in crossings:
            b, g, part = crossings[slot]
            stage["cross"] = packed(b.outer[g] if part else b.near[0][g])
        if slot in carries:
            b, g = carries[slot]
            stage["carry"] = b.inwards(g)
        if now(slot):
            piece = plan.pieces[slot]
            stage["fold"] = (piece, weight, came_pass[slot - LAG], side_of(piece))
        if now(slot + LAG):
            stage["send"] = inward(slot + LAG)
        index = slot - LAG
        if now(index):
            piece = plan.pieces[index]
            stage["merge"] = (
                piece,
                weight,
                came_pass[index - LAG],
                side_of(piece),
                came_mid[index],
                (other_parts, other_of(piece)),
            )
        index = slot - 2 * LAG
        if now(index):
            stage["gather"] = (plan.pieces[index],) + backs[slot - LAG]
        index = slot - 3 * LAG
        if now(index):
            stage["final"] = (
                plan.pieces[index],
                (sent_pass[slot - 2 * LAG], came_out[slot - 2 * LAG], 0),
                (sent_pass[slot - LAG], came_out[slot - LAG], sent_pass[slot - LAG].shape[0] - 1),
                buffer,
                full_acts if fused else None,
                result_total,
            )
        if slot in starts:
            b, turn = starts[slot]
            stage["ahead"] = (full_acts, weight, b.first, turn, ahead_total)
        got = slot_call(plan, flags, last, deps=deps, **stage)
        chain = [got[name] for name in ("across", "pass") if name in got][:1]
        if "across" in got:
            came_mid[slot] = send_mid(got["across"])
            backs[slot] = (came_mid[slot], got["across"].shape[0] - 1)
            if "back" in got:
                backs[slot] = (send_mid(got["back"]), 0)
        start_pass(slot, got)
        if "final" in got:
            buffer = got["final"]
            done = plan.pieces[slot - 3 * LAG]
            result_total = got.get("result")
            if done.first + done.units == plan.units:
                if fused:
                    out = result_total.astype(BF16)[None]
                else:
                    out = group_product(full_acts, buffer.reshape(plan.rows, plan.cols), done.group, 1)
                results.append(sum_rows(out).astype(BF16))
                result_total = None
        if "ahead" in got:
            ahead_total = got["ahead"]
            b, turn = starts[slot]
            if turn == AHEAD - 1:
                b.start(ahead_total.astype(BF16)[None])
                ahead_total = None
    result = jnp.moveaxis(jnp.concatenate(results), 0, 1).reshape(1, share, plan.cols)
    return buffer.reshape(plan.rows, plan.cols), result


def solution(mesh):
    placed = (
        P("task", "col", "row"),
        P("task", "row", "col"),
        P("task", None),
        P("task", None, "col"),
    )
    sizes = (mesh.shape["task"], mesh.shape["row"], mesh.shape["col"])
    return jax.shard_map(
        functools.partial(local, sizes),
        mesh=mesh,
        in_specs=placed,
        out_specs=(P("row", "col"), P("task", "row", "col")),
        check_vma=False,
    )
```

```python
import functools

import jax
import jax.numpy as jnp
from jax import lax
from jax.experimental import pallas as pl
from jax.experimental.pallas import tpu as pltpu
from jax.sharding import PartitionSpec as P

BF16 = jnp.bfloat16
F32 = jnp.float32
ANY = pl.BlockSpec(memory_space=pl.ANY)
WIDTH = 256
UNIT_ROWS = 384
MOST = 3
AHEAD = 3
LAG = 2
VMEM_LIMIT = 60 * 1024 * 1024
COST = pl.CostEstimate(flops=0, bytes_accessed=0, transcendentals=0)


def largest_divisor(total, limit, unit):
    best = total
    for size in range(unit, limit + 1, unit):
        if total % size == 0:
            best = size
    return best


def tie(arrays, deps):
    count = len(arrays)

    def body(*refs):
        pass

    return pl.pallas_call(
        body,
        out_shape=[jax.ShapeDtypeStruct(x.shape, x.dtype) for x in arrays],
        in_specs=[ANY] * (count + len(deps)),
        out_specs=[ANY] * count,
        input_output_aliases={i: i for i in range(count)},
        cost_estimate=COST,
        name="tie",
    )(*arrays, *deps)


def group_product(lhs, mat, group, groups, deps=()):
    tokens, rows = lhs.shape
    depth = largest_divisor(rows, 2304, 128)
    steps = rows // depth

    def body(lhs_ref, *rest):
        mats, (out_ref, acc_ref) = rest[:groups], rest[-2:]
        step = pl.program_id(0)
        wide = jnp.concatenate([mat[...] for mat in mats], axis=1) if groups > 1 else mats[0][...]
        part = jnp.dot(lhs_ref[...], wide, preferred_element_type=F32)

        @pl.when(step == 0)
        def _():
            acc_ref[...] = part

        @pl.when(step > 0)
        def _():
            acc_ref[...] += part

        @pl.when(step == steps - 1)
        def _():
            for g in range(groups):
                out_ref[g] = acc_ref[:, g * WIDTH : (g + 1) * WIDTH].astype(BF16)

    return pl.pallas_call(
        body,
        grid=(steps,),
        out_shape=jax.ShapeDtypeStruct((groups, tokens, WIDTH), BF16),
        in_specs=[pl.BlockSpec((tokens, depth), lambda k: (0, k))]
        + [pl.BlockSpec((depth, WIDTH), lambda k, g=g: (k, group + g)) for g in range(groups)]
        + [ANY] * len(deps),
        out_specs=pl.BlockSpec((groups, tokens, WIDTH), lambda k: (0, 0, 0)),
        scratch_shapes=[pltpu.VMEM((tokens, groups * WIDTH), F32)],
        compiler_params=pltpu.CompilerParams(vmem_limit_bytes=VMEM_LIMIT),
        cost_estimate=COST,
        name="group_product",
    )(lhs, *[mat] * groups, *deps)


def squares(acts, deps):
    tokens, rows = acts.shape
    depth = largest_divisor(rows, 768, 128)

    def body(acts_ref, *rest):
        wide = acts_ref[...].astype(F32)
        rest[-1][...] = (wide * wide).astype(BF16).T

    return pl.pallas_call(
        body,
        grid=(rows // depth,),
        out_shape=jax.ShapeDtypeStruct((rows, tokens), BF16),
        in_specs=[pl.BlockSpec((tokens, depth), lambda k: (0, k))] + [ANY] * len(deps),
        out_specs=pl.BlockSpec((depth, tokens), lambda k: (k, 0)),
        compiler_params=pltpu.CompilerParams(vmem_limit_bytes=VMEM_LIMIT),
        cost_estimate=COST,
        name="squares",
    )(acts, *deps)


class Piece:
    def __init__(self, group, first, units, place):
        self.group, self.first, self.units, self.place = group, first, units, place


class Plan:
    def __init__(self, rows, cols):
        self.rows, self.cols = rows, cols
        self.half = rows // 2
        self.groups = cols // WIDTH
        self.unit = largest_divisor(self.half, UNIT_ROWS, 16)
        self.units = self.half // self.unit
        lead = largest_divisor(self.units, MOST, 1)
        self.bounds = [(0, self.units)]
        self.pieces = []
        for group in range(self.groups):
            first = 0
            while first < self.units:
                left = self.units - first
                units = min(lead, left)
                self.pieces.append(Piece(group, first, units, len([p for p in self.pieces if p.group == group])))
                first += units

    def part_of(self, piece):
        q = [a <= piece.first < b for a, b in self.bounds].index(True)
        return q, piece.first - self.bounds[q][0]


def cut(plan, tasks, deps):
    unit, tokens = plan.unit, tasks[0].shape[0]
    parts = [b - a for a, b in plan.bounds]
    halves = sum(task.shape[1] // plan.half for task in tasks)
    steps = MOST
    if unit % 128 or any(part % steps for part in parts):
        wide = jnp.concatenate(tasks, axis=1).astype(F32)
        whole = (wide * wide).astype(BF16).T.reshape(halves, plan.half, tokens)
        return [whole[:, a * unit : b * unit] for a, b in plan.bounds]
    ins, in_specs, places = [], [], []
    count = 0
    for task in tasks:
        for h in range(task.shape[1] // plan.half):
            for q, (a, b) in enumerate(plan.bounds):
                per = (b - a) // steps
                for i in range(per):
                    first = h * plan.units + a + i
                    ins.append(task)
                    in_specs.append(
                        pl.BlockSpec((tokens, unit), lambda j, first=first, per=per: (0, first + per * j))
                    )
                    places.append((q, count, i))
            count += 1

    def body(*refs):
        outs = refs[len(refs) - len(parts) :]
        for ref, (q, h, i) in zip(refs, places):
            wide = ref[...].astype(F32)
            outs[q][h, i * unit : (i + 1) * unit] = (wide * wide).T.astype(BF16)

    return pl.pallas_call(
        body,
        grid=(steps,),
        out_shape=[jax.ShapeDtypeStruct((halves, part * unit, tokens), BF16) for part in parts],
        in_specs=in_specs + [ANY] * len(deps),
        out_specs=[
            pl.BlockSpec((halves, part // steps * unit, tokens), lambda j: (0, j, 0)) for part in parts
        ],
        compiler_params=pltpu.CompilerParams(vmem_limit_bytes=VMEM_LIMIT),
        cost_estimate=COST,
        name="cut",
    )(*ins, *deps)


def slot_call(plan, flags, last, fold=None, merge=None, gather=None, send=None, final=None, ahead=None, carry=None, cross=None, deps=()):
    unit = plan.unit
    ins, in_specs, outs, out_specs, aliases, kinds = [], [], [], [], {}, []
    most = lambda *some: max([part[0].units for part in some if part is not None] + [0])
    extra = lambda array: 0 if array is None else -(-array.shape[1] // unit)
    steps = max(
        most(final), most(merge, gather, send) + extra(carry), most(fold, merge) + extra(cross), 0 if ahead is None else AHEAD
    )

    def take(array, spec):
        ins.append(array)
        in_specs.append(spec)
        return len(ins) - 1

    def give(kind, shape, spec, dtype=BF16):
        outs.append(jax.ShapeDtypeStruct(shape, dtype))
        out_specs.append(spec)
        kinds.append(kind)
        return len(outs) - 1

    def at(piece, j):
        return jnp.minimum(j, piece.units - 1) if piece.units < steps else j

    def half_of(kind, flag):
        return {"sent": flag[0], "kept": 1 - flag[0]}.get(kind, kind)

    def rows_spec(piece, kind, width, column):
        return pl.BlockSpec(
            (unit, width),
            lambda j, flag: (half_of(kind, flag) * plan.units + piece.first + at(piece, j), column),
        )

    def half_spec(piece, kind):
        return pl.BlockSpec((None, unit, WIDTH), lambda j, flag: (half_of(kind, flag), at(piece, j), 0))

    def take_gsq(gsq, h):
        shape = (gsq.shape[0], None) + gsq.shape[2:]
        return take(gsq, pl.BlockSpec(shape, lambda j, flag: (0, h, 0, 0)))

    def give_long(kind, count, units, tail):
        total = units + extra(tail)
        last_block = total - 1
        out = give(
            kind,
            (count, units * unit + (0 if tail is None else tail.shape[1]), WIDTH),
            pl.BlockSpec((count, unit, WIDTH), lambda j, flag: (0, jnp.minimum(j, last_block), 0)),
        )
        if tail is None:
            return out, None
        blocks = extra(tail) - 1
        spec = pl.BlockSpec((2, unit, WIDTH), lambda j, flag: (0, jnp.clip(j - units, 0, blocks), 0))
        return out, (take(tail, spec), units, total)

    def take_side(piece, kind, tasks):
        ids = []
        squared, gsq = tasks
        for h, asq in enumerate(squared):
            if isinstance(asq, list):
                q, offset = plan.part_of(piece)
                array = asq[q]
                spec = pl.BlockSpec(
                    (array.shape[0], None, unit, array.shape[3]),
                    lambda j, flag: (0, half_of(kind, flag), offset + at(piece, j), 0),
                )
            else:
                array, spec = asq, rows_spec(piece, kind, asq.shape[1], 0)
            ids.append((take(array, spec), take_gsq(gsq, h)))
        return ids

    def take_other(piece, tasks):
        parts, gsq = tasks
        q, offset = plan.part_of(piece)
        array = parts[q]
        return [
            (
                take(
                    array,
                    pl.BlockSpec(
                        (array.shape[0], None, unit, array.shape[3]),
                        lambda j, flag, h=h: (0, h, offset + at(piece, j), 0),
                    ),
                ),
                take_gsq(gsq, h),
            )
            for h in range(gsq.shape[1])
        ]

    if fold is not None:
        piece, weight, received, side = fold
        fold_w = take(weight, rows_spec(piece, "sent", WIDTH, piece.group))
        fold_in = take(received, half_spec(piece, "sent"))
        fold_side = take_side(piece, "sent", side)
    if merge is not None:
        piece, weight, received, side, mean, other = merge
        merge_w = take(weight, rows_spec(piece, "kept", WIDTH, piece.group))
        merge_in = take(received, half_spec(piece, "kept"))
        merge_side = take_side(piece, "kept", side)
        merge_mean = take(mean, half_spec(piece, 0))
        merge_other = take_other(piece, other)
    apart = fold is not None and merge is not None and fold[0].units != merge[0].units
    if fold is not None or merge is not None:
        sections = 1 if fold is None or apart else 2
        across_out, across_tail = give_long("across", sections, most(merge if fold is None else fold), cross)
        back_out, back_place = across_out, sections - 1
        if apart:
            back_out, back_place = give_long("back", 1, most(merge), None)[0], 0
    outgoing = [part for part in (merge, gather) if part is not None]
    if outgoing or send is not None:
        if gather is not None:
            piece, came, section = gather
            gather_came = take(came, half_spec(piece, section))
        if send is not None:
            piece, inward, own = send
            if own:
                send_in = [take(inward, rows_spec(piece, h, WIDTH, piece.group)) for h in (0, 1)]
            else:
                send_in = [take(inward, half_spec(piece, h)) for h in (0, 1)]
        pass_count = 2 if send is not None or merge is not None else 1
        pass_out, pass_tail = give_long("pass", pass_count, most(merge, gather, send), carry)
    if final is not None:
        piece, kept, crossed, buffer, acts, total = final
        final_kept = [take(x, half_spec(piece, kept[2])) for x in kept[:2]]
        final_crossed = [take(x, half_spec(piece, crossed[2])) for x in crossed[:2]]
        first, group = piece.first, piece.group
        final_piece = piece
        final_out = give(
            "final",
            (2, plan.half, plan.cols),
            pl.BlockSpec((2, unit, WIDTH), lambda j, flag: (0, first + at(final_piece, j), group)),
        )
        if buffer is not None:
            aliases[1 + take(buffer, ANY)] = final_out
        if acts is not None:
            result_acts = [
                take(
                    acts,
                    pl.BlockSpec(
                        (acts.shape[0], unit),
                        lambda j, flag, h=h: (0, h * plan.units + first + at(final_piece, j)),
                    ),
                )
                for h in (0, 1)
            ]
            whole = pl.BlockSpec((acts.shape[0], WIDTH), lambda j, flag: (0, 0))
            result_in = None if total is None else take(total, whole)
            result_out = give("result", (acts.shape[0], WIDTH), whole, F32)
    if ahead is not None:
        ahead_acts, ahead_weight, ahead_group, ahead_turn, ahead_total = ahead
        tokens, depth = ahead_acts.shape[0], plan.rows // AHEAD**2
        block_at = lambda j: ahead_turn * AHEAD + jnp.minimum(j, AHEAD - 1)
        ahead_lhs = take(ahead_acts, pl.BlockSpec((tokens, depth), lambda j, flag: (0, block_at(j))))
        ahead_mat = take(ahead_weight, pl.BlockSpec((depth, WIDTH), lambda j, flag: (block_at(j), ahead_group)))
        everything = pl.BlockSpec((tokens, WIDTH), lambda j, flag: (0, 0))
        ahead_in = None if ahead_total is None else take(ahead_total, everything)
        ahead_out = give("ahead", (tokens, WIDTH), everything, F32)
    for dep in deps:
        take(dep, ANY)

    def body(flag, *refs):
        inr, outr = refs[: len(ins)], refs[len(ins) :]
        j = pl.program_id(0)

        def during(part, extra=True):
            units = part[0].units
            if units < steps:
                return pl.when((j < units) & extra)
            return pl.when(extra) if extra is not True else (lambda f: f())

        def fisher(task):
            ref = inr[task[0]]
            if len(ref.shape) == 3:
                asq = jnp.concatenate([ref[b] for b in range(ref.shape[0])], axis=1)
            else:
                asq = ref[...]
            gsq = inr[task[1]][...]
            return jnp.dot(asq, gsq.reshape(-1, gsq.shape[-1]), preferred_element_type=F32)

        def summed(tasks):
            return functools.reduce(lambda a, b: a + b, [fisher(task) for task in tasks])

        def follow(out, tail):
            ref, start, stop = tail

            @pl.when((j >= start) & (j < stop))
            def _():
                outr[out][...] = inr[ref][...]

        if carry is not None:
            follow(pass_out, pass_tail)
        if cross is not None:
            follow(across_out, across_tail)
        if send is not None:

            @during(send, flag[1] != last)
            def _():
                for h in (0, 1):
                    outr[pass_out][h] = inr[send_in[h]][...]

        if gather is not None:

            @during(gather, flag[1] == last)
            def _():
                outr[pass_out][pass_count - 1] = inr[gather_came][...]

        if final is not None:

            @during(final, flag[1] == last)
            def _():
                outr[final_out][1 - flag[0]] = inr[final_kept[0]][...]
                outr[final_out][flag[0]] = inr[final_crossed[0]][...]

            @during(final, flag[1] != last)
            def _():
                outr[final_out][1 - flag[0]] = inr[final_kept[1]][...]
                outr[final_out][flag[0]] = inr[final_crossed[1]][...]

        def add_to(out, before, value):
            @pl.when(j == 0)
            def _():
                outr[out][...] = value if before is None else inr[before][...] + value

            @pl.when(j > 0)
            def _():
                outr[out][...] += value

        if final is not None and final[4] is not None:

            @during(final)
            def _():
                parts = [
                    jnp.dot(inr[result_acts[h]][...], outr[final_out][h], preferred_element_type=F32)
                    for h in (0, 1)
                ]
                add_to(result_out, result_in, parts[0] + parts[1])

        if ahead is not None:

            @pl.when(j < AHEAD)
            def _():
                add_to(
                    ahead_out,
                    ahead_in,
                    jnp.dot(inr[ahead_lhs][...], inr[ahead_mat][...], preferred_element_type=F32),
                )

        if fold is not None:

            @during(fold)
            def _():
                here, before = fisher(fold_side[0]), summed(fold_side[1:])
                total = here + before
                mean = (here * inr[fold_w][...].astype(F32) + before * inr[fold_in][...].astype(F32)) / total
                outr[across_out][0] = jnp.where(total > 0, mean, 0.0).astype(BF16)

        if merge is not None:

            @during(merge)
            def _():
                here, before, there = fisher(merge_side[0]), summed(merge_side[1:]), summed(merge_other)
                numer = (
                    here * inr[merge_w][...].astype(F32)
                    + before * inr[merge_in][...].astype(F32)
                    + there * inr[merge_mean][...].astype(F32)
                )
                value = (numer / (here + before + there + 1e-6)).astype(BF16)
                outr[back_out][back_place] = value

                @pl.when(flag[1] == last)
                def _():
                    outr[pass_out][0] = value

    result = pl.pallas_call(
        body,
        grid_spec=pltpu.PrefetchScalarGridSpec(
            num_scalar_prefetch=1, grid=(steps,), in_specs=in_specs, out_specs=out_specs
        ),
        out_shape=outs,
        input_output_aliases=aliases,
        compiler_params=pltpu.CompilerParams(vmem_limit_bytes=VMEM_LIMIT),
        cost_estimate=COST,
        name="slot",
    )(flags, *ins)
    return dict(zip(kinds, result))


def local(sizes, activations, weights, labels, prototypes):
    tasks, rows_n, cols_n = sizes
    side_n = tasks // 2
    last = side_n - 1
    acts, weight, label_row, protos = activations[0], weights[0], labels[0], prototypes[0]
    block_tokens = acts.shape[0]
    tokens = block_tokens * cols_n
    share = tokens // rows_n
    plan = Plan(*weight.shape)
    place, row = lax.axis_index("task"), lax.axis_index("row")
    depth = jnp.minimum(place, tasks - 1 - place)
    sent = (place >= side_n).astype(jnp.int32)
    flags = jnp.stack([sent, depth.astype(jnp.int32)])

    mirrored = lambda pairs: pairs + [(tasks - 1 - a, tasks - 1 - b) for a, b in pairs]
    step_in = lambda d: mirrored([(d, d + 1)])
    step_out = lambda d: mirrored([(d + 1, d)])
    all_in = mirrored([(d, d + 1) for d in range(last)])
    send_in = lambda x: lax.ppermute(x, "task", all_in)
    send_mid = lambda x: lax.ppermute(x, "task", [(last, side_n), (side_n, last)])
    swap = lambda x: lax.ppermute(x, "task", step_in(last - 1) + step_out(last - 1))
    send_row = lambda x, s: lax.ppermute(x, "row", [(i, (i + s) % rows_n) for i in range(rows_n)])

    def sum_rows(full):
        cut_out = lambda r: lax.dynamic_slice_in_dim(full, r * share, share, 1)
        got = [send_row(cut_out((row + s) % rows_n), s) for s in range(1, rows_n)]
        total = cut_out(row).astype(F32)
        for part in got:
            total = total + part.astype(F32)
        return total

    def gather_rows(part):
        full = jnp.zeros((rows_n,) + part.shape, part.dtype)
        full = lax.dynamic_update_index_in_dim(full, part, row, 0)
        for s in range(1, rows_n):
            full = lax.dynamic_update_index_in_dim(full, send_row(part, s), (row - s) % rows_n, 0)
        return full

    full_acts = lax.all_gather(acts, "col", axis=0, tiled=True)

    crossing = lambda x: send_mid(lax.dynamic_slice_in_dim(x, sent * plan.half, plan.half, 1))
    near, cross = [acts], [crossing(acts)]
    for _ in range(last):
        near += tie([send_in(near[-1])], cross[-1:])
        cross.append(crossing(near[-1]))

    my_labels = lax.dynamic_slice_in_dim(label_row, row * share, share, 0)
    onehot = (my_labels[:, None] == lax.broadcasted_iota(jnp.int32, (share, protos.shape[0]), 1)).astype(BF16)
    target = jnp.dot(onehot, protos, preferred_element_type=F32)

    def squared_grad(product, group):
        groups = product.shape[0]
        wanted = target[:, group * WIDTH : (group + groups) * WIDTH].reshape(share, groups, WIDTH)
        grad = sum_rows(product) - jnp.moveaxis(wanted, 1, 0)
        return (grad * grad).astype(BF16)

    def packed(array):
        flat = array.reshape(-1, WIDTH)
        fill = -flat.shape[0] % 32
        return jnp.pad(flat, ((0, fill), (0, 0))).reshape(2, -1, WIDTH)

    def unpacked(array, shape):
        size = functools.reduce(lambda a, b: a * b, shape[:-1])
        rows = size + -size % 32
        return array[:, array.shape[1] - rows // 2 :].reshape(-1, WIDTH)[:size].reshape(shape)

    class Gradient:
        def __init__(self, group, groups):
            self.first, self.groups = group, groups
            self.outer, self.own, self.far, self.oth = ([None] * groups for _ in range(4))

        def start(self, product):
            self.near = [squared_grad(product, self.first)]
            for _ in range(last - 1):
                self.near.append(send_in(self.near[-1]))

        def inwards(self, g):
            return packed(jnp.stack([x[g] for x in self.near]))

        def inside(self, g, came):
            self.outer[g] = unpacked(came, (last, share, WIDTH))
            self.own[g] = gather_rows(jnp.concatenate([self.near[0][g][None], self.outer[g]]))

        def outside(self, g, part, came):
            came = unpacked(came, (last if part else 1, share, WIDTH))
            if part:
                self.oth[g] = gather_rows(jnp.concatenate([self.far[g], came]))
            else:
                self.far[g] = came

    count = len(plan.pieces)
    batches = [Gradient(0, 1)]
    while batches[-1].first + batches[-1].groups < plan.groups:
        group = batches[-1].first + batches[-1].groups
        batches.append(Gradient(group, 1))
    batch_of = {b.first + g: b for b in batches for g in range(b.groups)}
    own_of = lambda piece: batch_of[piece.group].own[piece.group - batch_of[piece.group].first]
    other_of = lambda piece: batch_of[piece.group].oth[piece.group - batch_of[piece.group].first]

    def inward(index):
        piece = plan.pieces[index]
        if last == 1:
            return (piece, weight, True)
        a, b = piece.first * plan.unit, (piece.first + piece.units) * plan.unit
        q, offset = plan.part_of(piece)
        offset *= plan.unit
        columns = slice(piece.group * WIDTH, (piece.group + 1) * WIDTH)
        mine = weight.reshape(2, plan.half, plan.cols)[:, a:b, columns]
        squared = [own_square.reshape(2, plan.half, tokens)[:, a:b]]
        for task in outer_parts[: last - 1]:
            blocks = task[q][:, :, offset : offset + b - a]
            squared.append(jnp.moveaxis(blocks, 0, 2).reshape(2, b - a, tokens))
        gsq = jnp.moveaxis(own_of(piece), 0, 1).reshape(side_n, tokens, WIDTH)
        shares = [
            jnp.einsum("hrt,tc->hrc", s, g, preferred_element_type=F32)
            for s, g in zip(squared, gsq)
        ]
        mean, before = mine, jnp.zeros(mine.shape, F32)
        for d in range(1, last):
            came = lax.ppermute(mean, "task", step_in(d - 1)).astype(F32)
            before = before + shares[d]
            total = shares[0] + before
            value = (shares[0] * mine.astype(F32) + before * came) / total
            mean = jnp.where(depth == 0, mine, jnp.where(total > 0, value, 0.0).astype(BF16))
        return (piece, mean, False)

    def outward(came):
        for d in reversed(range(last - 1)):
            arrived = lax.ppermute(came, "task", step_out(d))
            came = jnp.where(depth == d, arrived, came)
        return came

    sent_pass, came_pass, came_out = {}, {}, {}

    def start_pass(slot, got):
        if "pass" in got:
            sent_pass[slot] = got["pass"]
            came_pass[slot] = swap(got["pass"])
            came_out[slot] = outward(came_pass[slot])

    if last == 1:
        start_pass(-2, slot_call(plan, flags, last, send=inward(0), deps=[near[-1], cross[0]]))
    lead = batches[0]
    outer_cuts = [cut(plan, [task], list(sent_pass.values())) for task in near[1:]]
    rest = list(batches[1:])
    first_of = lambda b: min(i for i, p in enumerate(plan.pieces) if p.group == b.first)
    fused = last == 1 and plan.unit % 128 == 0 and plan.rows % (AHEAD**2 * 128) == 0
    fused = fused and all(first_of(b) >= AHEAD * (i + 1) for i, b in enumerate(rest))
    early = 1 + (min(LAG, len(rest)) if fused else len(rest))
    products = group_product(full_acts, weight, 0, early, deps=[x[0] for x in outer_cuts])
    gather_col = lambda x: lax.all_gather(x, "col", axis=0)
    outer_parts = [[gather_col(x) for x in task] for task in outer_cuts]

    def at_once(b, product):
        b.start(product)
        came = swap(jnp.stack(b.near))
        b.outer = [came[:, g] for g in range(b.groups)]
        stacked = jnp.concatenate([b.near[0][None], came])
        crossed = send_mid(stacked)
        b.own = [gather_rows(stacked[:, g]) for g in range(b.groups)]
        b.oth = [gather_rows(crossed[:, g]) for g in range(b.groups)]
        return crossed

    lead_far = at_once(lead, products[:1])
    own_square = squares(full_acts, [lead.near[0]])
    carries, crossings, starts = {}, {}, {}

    def ship(slot, b):
        for g in range(b.groups):
            carries[slot + g] = (b, g)
            crossings[slot + g] = (b, g, 0)
            crossings[slot + LAG + g] = (b, g, 1)

    if last == 1 and count > 1:
        start_pass(-1, slot_call(plan, flags, last, send=inward(1), deps=[own_square, lead.outer[0]] + list(came_pass.values())))
    other_cuts = cut(plan, cross, [own_square] + list(sent_pass.values())[-1:])
    other_parts = [gather_col(x) for x in other_cuts]
    if fused:
        for slot, b in enumerate(rest[:LAG]):
            b.start(products[1 + slot : 2 + slot])
            ship(slot, b)
        turn = 0
        for b in rest[LAG:]:
            starts.update({turn + k: (b, k) for k in range(AHEAD)})
            turn += AHEAD
            slot = turn
            while {slot, slot + LAG} & set(crossings):
                slot += 1
            ship(slot, b)
    else:
        for i, b in enumerate(rest):
            at_once(b, products[1 + i : 2 + i])
    if last > 1:
        for index in range(min(LAG, count)):
            start_pass(index - LAG, slot_call(plan, flags, last, send=inward(index)))

    came_mid, backs = {}, {}
    buffer = None
    results = []
    chain = [other_cuts[0], lead_far]
    ahead_total, result_total = None, None
    for slot in range(count + 3 * LAG):
        deps = list(chain)
        stage = {}
        now = lambda index: 0 <= index < count
        side_of = lambda piece: ([own_square] + outer_parts, own_of(piece))
        if slot - LAG in carries:
            b, g = carries[slot - LAG]
            b.inside(g, came_pass[slot - LAG])
        if slot - LAG in crossings:
            b, g, part = crossings[slot - LAG]
            b.outside(g, part, came_mid[slot - LAG])
        if slot in crossings:
            b, g, part = crossings[slot]
            stage["cross"] = packed(b.outer[g] if part else b.near[0][g])
        if slot in carries:
            b, g = carries[slot]
            stage["carry"] = b.inwards(g)
        if now(slot):
            piece = plan.pieces[slot]
            stage["fold"] = (piece, weight, came_pass[slot - LAG], side_of(piece))
        if now(slot + LAG):
            stage["send"] = inward(slot + LAG)
        index = slot - LAG
        if now(index):
            piece = plan.pieces[index]
            stage["merge"] = (
                piece,
                weight,
                came_pass[index - LAG],
                side_of(piece),
                came_mid[index],
                (other_parts, other_of(piece)),
            )
        index = slot - 2 * LAG
        if now(index):
            stage["gather"] = (plan.pieces[index],) + backs[slot - LAG]
        index = slot - 3 * LAG
        if now(index):
            stage["final"] = (
                plan.pieces[index],
                (sent_pass[slot - 2 * LAG], came_out[slot - 2 * LAG], 0),
                (sent_pass[slot - LAG], came_out[slot - LAG], sent_pass[slot - LAG].shape[0] - 1),
                buffer,
                full_acts if fused else None,
                result_total,
            )
        if slot in starts:
            b, turn = starts[slot]
            stage["ahead"] = (full_acts, weight, b.first, turn, ahead_total)
        got = slot_call(plan, flags, last, deps=deps, **stage)
        chain = [got[name] for name in ("across", "pass") if name in got][:1]
        if "across" in got:
            came_mid[slot] = send_mid(got["across"])
            backs[slot] = (came_mid[slot], got["across"].shape[0] - 1)
            if "back" in got:
                backs[slot] = (send_mid(got["back"]), 0)
        start_pass(slot, got)
        if "final" in got:
            buffer = got["final"]
            done = plan.pieces[slot - 3 * LAG]
            result_total = got.get("result")
            if done.first + done.units == plan.units:
                if fused:
                    out = result_total.astype(BF16)[None]
                else:
                    out = group_product(full_acts, buffer.reshape(plan.rows, plan.cols), done.group, 1)
                results.append(sum_rows(out).astype(BF16))
                result_total = None
        if "ahead" in got:
            ahead_total = got["ahead"]
            b, turn = starts[slot]
            if turn == AHEAD - 1:
                b.start(ahead_total.astype(BF16)[None])
                ahead_total = None
    result = jnp.moveaxis(jnp.concatenate(results), 0, 1).reshape(1, share, plan.cols)
    return buffer.reshape(plan.rows, plan.cols), result


def solution(mesh):
    placed = (
        P("task", "col", "row"),
        P("task", "row", "col"),
        P("task", None),
        P("task", None, "col"),
    )
    sizes = (mesh.shape["task"], mesh.shape["row"], mesh.shape["col"])
    return jax.shard_map(
        functools.partial(local, sizes),
        mesh=mesh,
        in_specs=placed,
        out_specs=(P("row", "col"), P("task", "row", "col")),
        check_vma=False,
    )
```
